32 devices in a mesh: chain: 4 (over y, x), gx: 2 (over core), gy: 4 (over z).
Axes of the slice: x: 2, y: 2, z: 4, core: 2. Of those that a mesh axis runs over, the one named last changes fastest.
Arguments:
- initial_path: float32 [8, 64, 96, 256], P('chain', 'gx', 'gy'), may hold values from -3 to 3, as said below
Outputs:
- relaxed_path: float32 [8, 64, 96, 256], P('chain', 'gx', 'gy')
The draws below stay inside these ranges and needn't reach their ends.
Inputs may be any that keep to these rules, and one draw needn't show every extreme that they name: `initial_path`: each image lies near a point of a path between the two end states, with image-to-image noise.
All inputs are finite; a program needn't handle non-finite values.
Results may differ from the reference program's by a relative error of at most 0.00013.
Values sent between devices are 32-bit elements; how exact they have to be, the bound alone decides.
No kernel may reach another device: no remote copies, remote signals or barrier semaphores. Data moves between devices by JAX's collectives and lax.ppermute only.
A program may use at most 64 MiB of HBM per device.

```python
import jax
import jax.numpy as jnp
from jax import lax

NZ = 256
RELAX = 3
OUTER = 1
IMAGES = 8
NX = 64
NY = 96


def draw_initial_path(key, part):
    ends_key = jax.random.fold_in(key, 11)
    gaps_key = jax.random.fold_in(key, 12)
    noise_key = jax.random.fold_in(key, 13)
    ends = -0.3 + 0.5 * jax.random.truncated_normal(ends_key, -4.0, 4.0, (2, NX, NY, NZ), jnp.float32)
    noise = 0.15 * jax.random.truncated_normal(noise_key, -4.0, 4.0, (IMAGES, NX, NY, NZ), jnp.float32)
    gaps = jax.random.uniform(gaps_key, (IMAGES - 1,), jnp.float32, 0.3, 1.7)
    position = jnp.concatenate([jnp.zeros((1,), jnp.float32), jnp.cumsum(gaps)]) / jnp.sum(gaps)
    weight = (4.0 * position * (1.0 - position))[:, None, None, None]
    shaped = position[:, None, None, None]
    return (1.0 - shaped) * ends[0][None] + shaped * ends[1][None] + weight * noise


def setup_inputs(seed: int = 0) -> dict:
    seeds = jax.random.split(jax.random.key(seed), 2)
    return {
        "initial_path": draw_initial_path(jax.random.fold_in(seeds[1], 71), 0),
    }


spacing = 0.7853981633974483
undercool = -0.25
time_step = 0.00025
step_size = 0.002
stiffness = 0.5
epsilon = 1e-06

def laplace(values):
    total = jnp.roll(values, -1, 0) + jnp.roll(values, 1, 0) + jnp.roll(values, -1, 1) + jnp.roll(values, 1, 1)
    total = total + jnp.roll(values, -1, 2) + jnp.roll(values, 1, 2)
    return (total - 6.0 * values) / (spacing * spacing)

def potential(field):
    first_lap = laplace(field)
    second_lap = laplace(first_lap)
    return (1.0 + undercool) * field + 2.0 * first_lap + second_lap + field * field * field

def relax_image(image):
    for relax_turn in range(RELAX):
        image = image + time_step * laplace(potential(image))
    return image

def reference(initial_path):
    field = initial_path
    cells = NX * NY * NZ
    for outer_turn in range(OUTER):
        field = lax.map(relax_image, field)
        chemical = lax.map(potential, field[1:-1])
        before = field[:-2]
        middle = field[1:-1]
        after = field[2:]
        tangent = after - before
        forward = after - middle
        backward = middle - before
        tangent_sq = lax.optimization_barrier(jnp.sum(tangent * tangent, axis=(1, 2, 3))) / cells
        forward_sq = lax.optimization_barrier(jnp.sum(forward * forward, axis=(1, 2, 3))) / cells
        backward_sq = lax.optimization_barrier(jnp.sum(backward * backward, axis=(1, 2, 3))) / cells
        intersection = lax.optimization_barrier(jnp.sum(chemical * tangent, axis=(1, 2, 3))) / cells
        scale = 1.0 / jnp.sqrt(tangent_sq + epsilon)
        unit = tangent * scale[:, None, None, None]
        along = intersection * scale
        spring = stiffness * (jnp.sqrt(forward_sq + epsilon) - jnp.sqrt(backward_sq + epsilon))
        moved = middle + step_size * (along[:, None, None, None] * unit - chemical) + spring[:, None, None, None] * unit
        field = jnp.concatenate([field[:1], moved, field[-1:]], axis=0)
    return field
```

```python
import functools

import jax
import jax.numpy as jnp
from jax import lax
from jax.experimental import pallas as pl
from jax.experimental.pallas import tpu as pltpu
from jax.sharding import PartitionSpec as P

RELAX = 3

spacing = 0.7853981633974483
undercool = -0.25
time_step = 0.00025
step_size = 0.002
stiffness = 0.5
epsilon = 1e-06

SUB = 8
LANES = 128
LAPS = 3
FIELD = LAPS * RELAX
REACH = FIELD + 2
CHUNKS = (11,)

VMEM = pl.BlockSpec(memory_space=pltpu.VMEM)
PARAMS = pltpu.CompilerParams(vmem_limit_bytes=32 << 20)


def neighbours(ref, i):
    c = ref[i]
    up = jnp.concatenate([c[1:], pltpu.roll(c[:1], SUB - 1, 1)], axis=0)
    down = jnp.concatenate([pltpu.roll(c[-1:], 1, 1), c[:-1]], axis=0)
    nz = c.shape[-1]
    side = pltpu.roll(c, 1, 2) + pltpu.roll(c, nz - 1, 2)
    return (ref[i - 1] + ref[i + 1]) + (up + down) + side - 6.0 * c


def potential_row(v, w, d):
    h2 = spacing * spacing
    return v * ((1.0 + undercool) + v * v) + (2.0 / h2) * w + (1.0 / (h2 * h2)) * d


def context(m):
    return LAPS if m % LAPS == 0 else 2


def level_row(levels, m, y):
    below, off = levels[m - 1]
    d = neighbours(below, y + off)
    kind = m % LAPS
    if kind == 1:
        return d
    w = below[y + off]
    ref, off = levels[m - 2 if kind == 2 else m - LAPS]
    v = ref[y + off]
    if kind == 2:
        return potential_row(v, w, d)
    return v + (time_step / (spacing * spacing)) * d


def rows_of(levels, m, start, stop, into):
    count = stop[0] - start[0]

    def body(i, carry):
        for side in range(2):
            ref, off = into[side]
            y = start[side] + i
            ref[y + off] = level_row(levels[side], m, y)
        return carry

    lax.fori_loop(0, count, body, 0)


def first_kernel(rows, sends, who_ref, whole_ref, recv_ref, *refs):
    slab, pieces = refs[0], refs[1:-2]
    halves, sems = refs[-2:]
    _, tiles, half, _, lanes = halves.shape
    planes = 2 * half // SUB
    copies = []
    for i, src in enumerate((whole_ref.at[who_ref[0]], recv_ref)):
        for z in range(tiles):
            part = src.at[:, :, pl.ds(z * lanes, lanes)]
            copies.append(pltpu.make_async_copy(part, halves.at[i, z], sems.at[i, z]))
    for copy in copies:
        copy.start()
    for copy in copies:
        copy.wait()
    flat = halves.reshape(2, tiles, half * rows, lanes)
    h = SUB // 2

    def body(y, carry):
        for r in range(planes):
            where = pl.ds(r * rows + y, h, stride=planes * rows)
            for i in range(2):
                for z in range(tiles):
                    slab[y, r, i * h : i * h + h, z * lanes : (z + 1) * lanes] = flat[i, z, where, :]
        return carry

    lax.fori_loop(0, rows, body, 0)
    for piece, (start, count) in zip(pieces, sends):
        def copy(i, carry, piece=piece, start=start):
            piece[i] = slab[start + i]
            return carry

        lax.fori_loop(0, count, copy, 0)


def inner_kernel(rows, slab_ref, *outs):
    levels = [(slab_ref, 0)] + [(ref, -m) for m, ref in enumerate(outs, 1)]
    for m in range(1, FIELD + 1):
        count = (rows - 2 * m) // 2
        start, stop = (m, m + count), (m + count, rows - m)
        rows_of((levels, levels), m, start, stop, (levels[m], levels[m]))


def edge_kernel(rows, before, after, low_ref, high_ref, *refs):
    count = after - before
    past, levels = refs[:FIELD], refs[-FIELD:]
    fields = refs[FIELD:-FIELD]
    sides = ([], [])
    for m, (old, new) in enumerate(zip(past, levels)):
        c = context(m)
        total = count + c
        for i in range(c):
            new[count + i] = old[i]
            new[total + i] = old[old.shape[0] - c + i]
        sides[0].append((new, after - m))
        sides[1].append((new, total + c - (rows - m + before)))

    def fill(i, carry):
        levels[0][i] = low_ref[i]
        levels[0][count + 2 * context(0) + i] = high_ref[i]
        return carry

    lax.fori_loop(0, count, fill, 0)
    for m in range(1, FIELD):
        start = (m - after, rows - m + before)
        stop = (m - before, rows - m + after)
        rows_of(sides, m, start, stop, (sides[0][m], sides[1][m]))
    beyond = max(0, after - FIELD)
    kept = count - beyond
    if kept:
        low = FIELD - after + beyond
        high = rows - FIELD + before
        into = ((fields[0], -low), (fields[0], kept - high))
        rows_of(sides, FIELD, (low, high), (low + kept, high + kept), into)
    if beyond:
        into = ((fields[-1], beyond), (fields[-1], beyond - rows))
        rows_of(sides, FIELD, (-beyond, rows), (0, rows + beyond), into)


def end_kernel(rows, segments, keep_ref, halo_ref, *refs):
    n = len(segments)
    pieces, partners, chains = refs[:n], refs[n : 2 * n], refs[2 * n : 3 * n]
    mine_ref, send_ref, sums_ref, field_ref, w_ref = refs[3 * n :]
    keep = keep_ref[0] != 0
    planes, nz = field_ref.shape[1], field_ref.shape[3]
    lanes = mine_ref.shape[-1]
    for i in range(2):
        field_ref[i] = halo_ref[i]
        field_ref[rows + 2 + i] = halo_ref[2 + i]
    for parts, piece in zip(segments, pieces):
        for start, count, first in parts:
            def copy(i, carry, start=start, first=first, piece=piece):
                field_ref[2 + start + i] = piece[first + i]
                return carry

            lax.fori_loop(0, count, copy, 0)

    def lap(i, carry):
        w_ref[i] = neighbours(field_ref, i + 1)
        return carry

    lax.fori_loop(0, rows + 2, lap, 0)
    sums_ref[...] = jnp.zeros_like(sums_ref)

    def fold(a):
        return sum(a[r, :, z : z + 128] for r in range(planes) for z in range(0, nz, lanes))

    def row(y, i, partner, chain):
        f = field_ref[y + 2]
        chem = potential_row(f, w_ref[y + 1], neighbours(w_ref, y + 1))
        a, b = partner[i], chain[i]
        t = a - b
        fr = pltpu.roll(f, SUB // 2, 1)
        da, db = a - fr, b - fr
        cr = pltpu.roll(chem, SUB // 2, 1)
        sums_ref[0] += fold(t * t)
        sums_ref[1] += fold(da * da)
        sums_ref[2] += fold(db * db)
        sums_ref[3] += fold(cr * t)
        g = jnp.where(keep, f, f - step_size * chem)
        h = SUB // 2
        for r in range(planes):
            where = pl.ds(r * rows + y, h, stride=planes * rows)
            for z in range(nz // lanes):
                at = slice(z * lanes, (z + 1) * lanes)
                mine_ref[0, z, where, :] = g[r, :h, at]
                send_ref[0, z, where, :] = g[r, h:, at]
                mine_ref[1, z, where, :] = t[r, h:, at]
                send_ref[1, z, where, :] = t[r, :h, at]

    for parts, partner, chain in zip(segments, partners, chains):
        for start, count, first in parts:
            def body(i, carry, start=start, first=first, partner=partner, chain=chain):
                row(start + i, first + i, partner, chain)
                return carry

            lax.fori_loop(0, count, body, 0)


def last_kernel(cells, keep_ref, who_ref, sums_ref, mine_ref, recv_ref, out_ref):
    def factor(i):
        def total(q):
            return jnp.sum(sums_ref[i, q], keepdims=True) / cells

        scale = lax.rsqrt(total(0) + epsilon)
        spring = stiffness * (jnp.sqrt(total(1) + epsilon) - jnp.sqrt(total(2) + epsilon))
        k = step_size * total(3) * scale * scale + spring * scale
        return jnp.where(keep_ref[i] != 0, jnp.zeros_like(k), k)

    _, half, rows, _ = out_ref.shape
    _, tiles, _, lanes = mine_ref.shape
    for i, ref in enumerate((mine_ref, recv_ref)):
        k = factor(i)
        image = who_ref[0] if i == 0 else 1 - who_ref[0]
        for z in range(tiles):
            value = ref[0, z] + k * ref[1, z]
            out_ref[image, :, :, z * lanes : (z + 1) * lanes] = value.reshape(half, rows, lanes)


def ring(axis, distance):
    n = lax.axis_size(axis)
    return [(i, (i + distance) % n) for i in range(n)]


def total_over(value, axis):
    n = lax.axis_size(axis)
    if n & (n - 1):
        return value + sum(lax.ppermute(value, axis, ring(axis, d)) for d in range(1, n))
    d = 1
    while d < n:
        value = value + lax.ppermute(value, axis, [(i, i ^ d) for i in range(n)])
        d *= 2
    return value


def per_device(initial_path):
    count, half, rows, nz = initial_path.shape
    assert count == lax.axis_size("gx") == 2
    assert rows % 2 == 0 and rows >= 2 * REACH and half % SUB == 0 and nz % LANES == 0
    planes = 2 * half // SUB
    cells = 2 * half * rows * lax.axis_size("gy") * nz
    chains = lax.axis_size("chain")
    gx = lax.axis_index("gx")
    chain = lax.axis_index("chain")
    swap = [(0, 1), (1, 0)]
    tiles = nz // LANES
    smem = pl.BlockSpec(memory_space=pltpu.SMEM)

    def slab(n):
        return jax.ShapeDtypeStruct((n, planes, SUB, nz), jnp.float32)

    who = gx.astype(jnp.int32)[None]
    other = lax.dynamic_index_in_dim(initial_path, 1 - gx, 0, keepdims=False)
    recv = lax.ppermute(other, "gx", swap)
    known = [0]
    for n in CHUNKS:
        known.append(known[-1] + n)
    sends = []
    for a, b in zip(known, known[1:]):
        sends += [(a, b - a), (rows - b, b - a)]
    first = pl.pallas_call(
        functools.partial(first_kernel, rows, sends),
        out_shape=[slab(rows)] + [slab(n) for _, n in sends],
        in_specs=[smem, pl.BlockSpec(memory_space=pl.ANY), pl.BlockSpec(memory_space=pl.ANY)],
        out_specs=[VMEM] * (1 + len(sends)),
        scratch_shapes=[
            pltpu.VMEM((2, tiles, half, rows, LANES), jnp.float32),
            pltpu.SemaphoreType.DMA((2, tiles)),
        ],
        compiler_params=PARAMS,
        name="first",
    )(who, initial_path, recv)
    halos = []
    for j in range(len(CHUNKS)):
        low, high = first[1 + 2 * j], first[2 + 2 * j]
        halos.append((
            lax.ppermute(high, "gy", ring("gy", 1)),
            lax.ppermute(low, "gy", ring("gy", -1)),
        ))

    inner = pl.pallas_call(
        functools.partial(inner_kernel, rows),
        out_shape=[slab(rows - 2 * m) for m in range(1, FIELD + 1)],
        in_specs=[VMEM],
        out_specs=[VMEM] * FIELD,
        compiler_params=PARAMS,
        name="inner",
    )(first[0])
    levels = [first[0]] + list(inner[:-1])
    pieces = [inner[-1]]
    segments = [[(FIELD, rows - 2 * FIELD, 0)]]
    for (low, high), a, b in zip(halos, known, known[1:]):
        beyond = max(0, b - FIELD)
        kept = b - a - beyond
        fields = [slab(2 * n) for n in (kept, beyond) if n]
        buffers = [(2 * (b - a + context(m)), planes, SUB, nz) for m in range(FIELD)]
        last = b == REACH
        outs = fields if last else fields + [slab(shape[0]) for shape in buffers]
        done = pl.pallas_call(
            functools.partial(edge_kernel, rows, a, b),
            out_shape=outs,
            in_specs=[VMEM] * (FIELD + 2),
            out_specs=[VMEM] * len(outs),
            scratch_shapes=[pltpu.VMEM(shape, jnp.float32) for shape in buffers] if last else [],
            compiler_params=PARAMS,
            name="edge",
        )(low, high, *levels)
        if kept:
            pieces.append(done[0])
            segments.append([(FIELD - a - kept, kept, 0), (rows - FIELD + a, kept, kept)])
        levels = list(done[len(fields) :])
        halo = done[len(fields) - 1]

    along_chain = []
    for c in range(chains - 1):
        along_chain += [(2 * c + 1, 2 * c + 2), (2 * c + 2, 2 * c + 1)]
    from_partner = [lax.ppermute(p, "gx", swap) for p in pieces]
    from_chain = [lax.ppermute(p, ("chain", "gx"), along_chain) for p in pieces]

    def keeping(image):
        return jnp.logical_or(image == 0, image == 2 * chains - 1).astype(jnp.int32)

    keep = jnp.stack([keeping(2 * chain + gx), keeping(2 * chain + 1 - gx)])
    part = jax.ShapeDtypeStruct((2, tiles, half * rows, LANES), jnp.float32)
    mine, send, sums = pl.pallas_call(
        functools.partial(end_kernel, rows, segments),
        out_shape=[part, part, jax.ShapeDtypeStruct((4, SUB, LANES), jnp.float32)],
        in_specs=[smem] + [VMEM] * (1 + 3 * len(pieces)),
        out_specs=[VMEM] * 3,
        scratch_shapes=[
            pltpu.VMEM((rows + 4, planes, SUB, nz), jnp.float32),
            pltpu.VMEM((rows + 2, planes, SUB, nz), jnp.float32),
        ],
        compiler_params=PARAMS,
        name="end",
    )(keep, halo, *pieces, *from_partner, *from_chain)
    halfway = lax.ppermute(send, "gx", swap)
    total = total_over(sums, "gy")
    totals = jnp.stack([total, lax.ppermute(total, "gx", swap)])
    return pl.pallas_call(
        functools.partial(last_kernel, cells),
        out_shape=jax.ShapeDtypeStruct(initial_path.shape, jnp.float32),
        in_specs=[smem, smem] + [VMEM] * 3,
        out_specs=VMEM,
        compiler_params=PARAMS,
        name="last",
    )(keep, who, totals, mine, halfway)


def solution(mesh):
    return jax.shard_map(
        per_device,
        mesh=mesh,
        in_specs=(P("chain", "gx", "gy", None),),
        out_specs=P("chain", "gx", "gy", None),
        check_vma=False,
    )
```

```python
import functools

import jax
import jax.numpy as jnp
from jax import lax
from jax.experimental import pallas as pl
from jax.experimental.pallas import tpu as pltpu
from jax.sharding import PartitionSpec as P

RELAX = 3

spacing = 0.7853981633974483
undercool = -0.25
time_step = 0.00025
step_size = 0.002
stiffness = 0.5
epsilon = 1e-06

SUB = 8
LANES = 128
LAPS = 3
FIELD = LAPS * RELAX
REACH = FIELD + 2
CHUNKS = (5, 4, 2)

VMEM = pl.BlockSpec(memory_space=pltpu.VMEM)
PARAMS = pltpu.CompilerParams(vmem_limit_bytes=8 << 20)


def neighbours(ref, i):
    c = ref[i]
    up = jnp.concatenate([c[1:], pltpu.roll(c[:1], SUB - 1, 1)], axis=0)
    down = jnp.concatenate([pltpu.roll(c[-1:], 1, 1), c[:-1]], axis=0)
    nz = c.shape[-1]
    side = pltpu.roll(c, 1, 2) + pltpu.roll(c, nz - 1, 2)
    return (ref[i - 1] + ref[i + 1]) + (up + down) + side - 6.0 * c


def potential_row(v, w, d):
    h2 = spacing * spacing
    return v * ((1.0 + undercool) + v * v) + (2.0 / h2) * w + (1.0 / (h2 * h2)) * d


def context(m):
    return LAPS if m % LAPS == 0 else 2


def level_row(levels, m, y):
    below, off = levels[m - 1]
    d = neighbours(below, y + off)
    kind = m % LAPS
    if kind == 1:
        return d
    w = below[y + off]
    ref, off = levels[m - 2 if kind == 2 else m - LAPS]
    v = ref[y + off]
    if kind == 2:
        return potential_row(v, w, d)
    return v + (time_step / (spacing * spacing)) * d


def rows_of(levels, m, start, stop, into):
    for i in range(stop[0] - start[0]):
        for side in range(2):
            ref, off = into[side]
            y = start[side] + i
            ref[y + off] = level_row(levels[side], m, y)


def first_kernel(rows, sends, who_ref, whole_ref, recv_ref, *refs):
    slab, pieces = refs[0], refs[1:-2]
    halves, sems = refs[-2:]
    _, tiles, half, _, lanes = halves.shape
    planes = 2 * half // SUB
    copies = []
    for i, src in enumerate((whole_ref.at[who_ref[0]], recv_ref)):
        for z in range(tiles):
            part = src.at[:, :, pl.ds(z * lanes, lanes)]
            copies.append(pltpu.make_async_copy(part, halves.at[i, z], sems.at[i, z]))
    for copy in copies:
        copy.start()
    for copy in copies:
        copy.wait()
    flat = halves.reshape(2, tiles, half * rows, lanes)
    h = SUB // 2

    def body(y, carry):
        for r in range(planes):
            where = pl.ds(r * rows + y, h, stride=planes * rows)
            for i in range(2):
                for z in range(tiles):
                    slab[y, r, i * h : i * h + h, z * lanes : (z + 1) * lanes] = flat[i, z, where, :]
        return carry

    lax.fori_loop(0, rows, body, 0)
    for piece, (start, count) in zip(pieces, sends):
        def copy(i, carry, piece=piece, start=start):
            piece[i] = slab[start + i]
            return carry

        lax.fori_loop(0, count, copy, 0)


def inner_kernel(rows, slab_ref, *outs):
    levels = [(slab_ref, 0)] + [(ref, -m) for m, ref in enumerate(outs, 1)]
    for m in range(1, FIELD + 1):
        count = (rows - 2 * m) // 2
        start, stop = (m, m + count), (m + count, rows - m)
        rows_of((levels, levels), m, start, stop, (levels[m], levels[m]))


def edge_kernel(rows, before, after, low_ref, high_ref, *refs):
    count = after - before
    past, levels = refs[:FIELD], refs[-FIELD:]
    fields = refs[FIELD:-FIELD]
    sides = ([], [])
    for m, (old, new) in enumerate(zip(past, levels)):
        c = context(m)
        total = count + c
        for i in range(c):
            new[count + i] = old[i]
            new[total + i] = old[old.shape[0] - c + i]
        sides[0].append((new, after - m))
        sides[1].append((new, total + c - (rows - m + before)))

    def fill(i, carry):
        levels[0][i] = low_ref[i]
        levels[0][count + 2 * context(0) + i] = high_ref[i]
        return carry

    lax.fori_loop(0, count, fill, 0)
    for m in range(1, FIELD):
        start = (m - after, rows - m + before)
        stop = (m - before, rows - m + after)
        rows_of(sides, m, start, stop, (sides[0][m], sides[1][m]))
    beyond = max(0, after - FIELD)
    kept = count - beyond
    if kept:
        low = FIELD - after + beyond
        high = rows - FIELD + before
        into = ((fields[0], -low), (fields[0], kept - high))
        rows_of(sides, FIELD, (low, high), (low + kept, high + kept), into)
    if beyond:
        into = ((fields[-1], beyond), (fields[-1], beyond - rows))
        rows_of(sides, FIELD, (-beyond, rows), (0, rows + beyond), into)


def chemical_kernel(rows, segments, halo_ref, *refs):
    n = len(segments)
    pieces, outs = refs[:n], refs[n : 2 * n]
    field_ref, w_ref = refs[2 * n :]
    for i in range(2):
        field_ref[i] = halo_ref[i]
        field_ref[rows + 2 + i] = halo_ref[2 + i]
    for parts, piece in zip(segments, pieces):
        for start, count, first in parts:
            for i in range(count):
                field_ref[2 + start + i] = piece[first + i]
    for i in range(rows + 2):
        w_ref[i] = neighbours(field_ref, i + 1)
    for parts, out in zip(segments, outs):
        for start, count, first in parts:
            for i in range(count):
                y = start + i
                out[first + i] = potential_row(field_ref[y + 2], w_ref[y + 1], neighbours(w_ref, y + 1))


def sums_kernel(n, lanes, keep_ref, *refs):
    sums_ref, outs = refs[4 * n], refs[4 * n + 1 :]
    keep = keep_ref[0] != 0
    planes, nz = refs[0].shape[1], refs[0].shape[3]

    def fold(a):
        return sum(a[r, :, z : z + lanes] for r in range(planes) for z in range(0, nz, lanes))

    low = lax.broadcasted_iota(jnp.int32, (planes, SUB, nz), 1) < SUB // 2
    totals = [jnp.zeros((SUB, lanes), jnp.float32)] * 4
    for j in range(n):
        piece, partner, chain, chemical = refs[j : 4 * n : n]
        mine, send = outs[2 * j], outs[2 * j + 1]

        def body(i, totals, piece=piece, partner=partner, chain=chain, chemical=chemical, mine=mine, send=send):
            f, a, b, chem = piece[i], partner[i], chain[i], chemical[i]
            t = a - b
            fr = pltpu.roll(f, SUB // 2, 1)
            cr = pltpu.roll(chem, SUB // 2, 1)
            da, db = a - fr, b - fr
            g = jnp.where(keep, f, f - step_size * chem)
            mine[i] = jnp.where(low, g, t)
            send[i] = jnp.where(low, t, g)
            parts = (fold(t * t), fold(da * da), fold(db * db), fold(cr * t))
            return tuple(total + part for total, part in zip(totals, parts))

        totals = lax.fori_loop(0, piece.shape[0], body, tuple(totals))
    for q in range(4):
        sums_ref[q] = totals[q]


def last_kernel(cells, segments, keep_ref, who_ref, sums_ref, *refs):
    n = len(segments)
    out_ref, natural, sems = refs[2 * n :]
    _, half, rows, _ = out_ref.shape
    _, tiles, _, _, lanes = natural.shape
    flat = natural.reshape(2, tiles, half * rows, lanes)
    planes = 2 * half // SUB
    h = SUB // 2

    def factor(i):
        def total(q):
            return jnp.sum(sums_ref[i, q], keepdims=True) / cells

        scale = lax.rsqrt(total(0) + epsilon)
        spring = stiffness * (jnp.sqrt(total(1) + epsilon) - jnp.sqrt(total(2) + epsilon))
        k = step_size * total(3) * scale * scale + spring * scale
        return jnp.where(keep_ref[i] != 0, jnp.zeros_like(k), k)

    copies = []
    for i in range(2):
        k = factor(i)
        image = who_ref[0] if i == 0 else 1 - who_ref[0]
        for parts, ref in zip(segments, refs[i * n : (i + 1) * n]):
            for start, count, first in parts:
                def body(j, carry, start=start, first=first, ref=ref, i=i, k=k):
                    for r in range(planes):
                        for z in range(tiles):
                            at = slice(z * lanes, (z + 1) * lanes)
                            v = ref[first + j, r, :, at]
                            v = v + k * pltpu.roll(v, h, 0)
                            where = pl.ds(r * rows + start + j, h, stride=planes * rows)
                            flat[i, z, where, :] = v[i * h : i * h + h]
                    return carry

                lax.fori_loop(0, count, body, 0)
        for z in range(tiles):
            part = out_ref.at[image, :, :, pl.ds(z * lanes, lanes)]
            copies.append(pltpu.make_async_copy(natural.at[i, z], part, sems.at[i, z]))
            copies[-1].start()
    for copy in copies:
        copy.wait()


def ring(axis, distance):
    n = lax.axis_size(axis)
    return [(i, (i + distance) % n) for i in range(n)]


def total_over(value, axis):
    n = lax.axis_size(axis)
    if n & (n - 1):
        return value + sum(lax.ppermute(value, axis, ring(axis, d)) for d in range(1, n))
    d = 1
    while d < n:
        value = value + lax.ppermute(value, axis, [(i, i ^ d) for i in range(n)])
        d *= 2
    return value


def per_device(initial_path):
    count, half, rows, nz = initial_path.shape
    assert count == lax.axis_size("gx") == 2
    assert rows % 2 == 0 and rows >= 2 * REACH and half % SUB == 0 and nz % LANES == 0
    planes = 2 * half // SUB
    cells = 2 * half * rows * lax.axis_size("gy") * nz
    chains = lax.axis_size("chain")
    gx = lax.axis_index("gx")
    chain = lax.axis_index("chain")
    swap = [(0, 1), (1, 0)]
    tiles = nz // LANES
    smem = pl.BlockSpec(memory_space=pltpu.SMEM)

    def slab(n):
        return jax.ShapeDtypeStruct((n, planes, SUB, nz), jnp.float32)

    who = gx.astype(jnp.int32)[None]
    other = lax.dynamic_index_in_dim(initial_path, 1 - gx, 0, keepdims=False)
    recv = lax.ppermute(other, "gx", swap)
    known = [0]
    for n in CHUNKS:
        known.append(known[-1] + n)
    sends = []
    for a, b in zip(known, known[1:]):
        sends += [(a, b - a), (rows - b, b - a)]
    first = pl.pallas_call(
        functools.partial(first_kernel, rows, sends),
        out_shape=[slab(rows)] + [slab(n) for _, n in sends],
        in_specs=[smem, pl.BlockSpec(memory_space=pl.ANY), pl.BlockSpec(memory_space=pl.ANY)],
        out_specs=[VMEM] * (1 + len(sends)),
        scratch_shapes=[
            pltpu.VMEM((2, tiles, half, rows, LANES), jnp.float32),
            pltpu.SemaphoreType.DMA((2, tiles)),
        ],
        compiler_params=PARAMS,
        name="first",
    )(who, initial_path, recv)
    halos = []
    for j in range(len(CHUNKS)):
        low, high = first[1 + 2 * j], first[2 + 2 * j]
        halos.append((
            lax.ppermute(high, "gy", ring("gy", 1)),
            lax.ppermute(low, "gy", ring("gy", -1)),
        ))

    inner = pl.pallas_call(
        functools.partial(inner_kernel, rows),
        out_shape=[slab(rows - 2 * m) for m in range(1, FIELD + 1)],
        in_specs=[VMEM],
        out_specs=[VMEM] * FIELD,
        compiler_params=PARAMS,
        name="inner",
    )(first[0])
    levels = [first[0]] + list(inner[:-1])
    pieces = [inner[-1]]
    segments = [[(FIELD, rows - 2 * FIELD, 0)]]
    for (low, high), a, b in zip(halos, known, known[1:]):
        beyond = max(0, b - FIELD)
        kept = b - a - beyond
        fields = [slab(2 * n) for n in (kept, beyond) if n]
        buffers = [(2 * (b - a + context(m)), planes, SUB, nz) for m in range(FIELD)]
        last = b == REACH
        outs = fields if last else fields + [slab(shape[0]) for shape in buffers]
        done = pl.pallas_call(
            functools.partial(edge_kernel, rows, a, b),
            out_shape=outs,
            in_specs=[VMEM] * (FIELD + 2),
            out_specs=[VMEM] * len(outs),
            scratch_shapes=[pltpu.VMEM(shape, jnp.float32) for shape in buffers] if last else [],
            compiler_params=PARAMS,
            name="edge",
        )(low, high, *levels)
        if kept:
            pieces.append(done[0])
            segments.append([(FIELD - a - kept, kept, 0), (rows - FIELD + a, kept, kept)])
        levels = list(done[len(fields) :])
        halo = done[len(fields) - 1]

    along_chain = []
    for c in range(chains - 1):
        along_chain += [(2 * c + 1, 2 * c + 2), (2 * c + 2, 2 * c + 1)]
    from_partner = [lax.ppermute(p, "gx", swap) for p in pieces]
    from_chain = [lax.ppermute(p, ("chain", "gx"), along_chain) for p in pieces]

    def keeping(image):
        return jnp.logical_or(image == 0, image == 2 * chains - 1).astype(jnp.int32)

    keep = jnp.stack([keeping(2 * chain + gx), keeping(2 * chain + 1 - gx)])
    chemical = pl.pallas_call(
        functools.partial(chemical_kernel, rows, segments),
        out_shape=[slab(p.shape[0]) for p in pieces],
        in_specs=[VMEM] * (1 + len(pieces)),
        out_specs=[VMEM] * len(pieces),
        scratch_shapes=[
            pltpu.VMEM((rows + 4, planes, SUB, nz), jnp.float32),
            pltpu.VMEM((rows + 2, planes, SUB, nz), jnp.float32),
        ],
        compiler_params=PARAMS,
        name="chemical",
    )(halo, *pieces)
    mine, halfway, total = [], [], 0.0
    for some in (slice(0, -1), slice(-1, None)):
        n = len(pieces[some])
        sums, *outs = pl.pallas_call(
            functools.partial(sums_kernel, n, LANES),
            out_shape=[jax.ShapeDtypeStruct((4, SUB, LANES), jnp.float32)]
            + [slab(p.shape[0]) for p in pieces[some] for _ in range(2)],
            in_specs=[smem] + [VMEM] * (4 * n),
            out_specs=[VMEM] * (1 + 2 * n),
            compiler_params=PARAMS,
            name="sums",
        )(keep, *pieces[some], *from_partner[some], *from_chain[some], *chemical[some])
        total = total + sums
        mine += outs[::2]
        halfway += [lax.ppermute(send, "gx", swap) for send in outs[1::2]]
    total = total_over(total, "gy")
    totals = jnp.stack([total, lax.ppermute(total, "gx", swap)])
    return pl.pallas_call(
        functools.partial(last_kernel, cells, segments),
        out_shape=jax.ShapeDtypeStruct(initial_path.shape, jnp.float32),
        in_specs=[smem, smem] + [VMEM] * (1 + 2 * len(pieces)),
        out_specs=pl.BlockSpec(memory_space=pl.ANY),
        scratch_shapes=[
            pltpu.VMEM((2, tiles, half, rows, LANES), jnp.float32),
            pltpu.SemaphoreType.DMA((2, tiles)),
        ],
        compiler_params=PARAMS,
        name="last",
    )(keep, who, totals, *mine, *halfway)


def solution(mesh):
    return jax.shard_map(
        per_device,
        mesh=mesh,
        in_specs=(P("chain", "gx", "gy", None),),
        out_specs=P("chain", "gx", "gy", None),
        check_vma=False,
    )
```

```python
import functools

import jax
import jax.numpy as jnp
from jax import lax
from jax.experimental import pallas as pl
from jax.experimental.pallas import tpu as pltpu
from jax.sharding import PartitionSpec as P

RELAX = 3

spacing = 0.7853981633974483
undercool = -0.25
time_step = 0.00025
step_size = 0.002
stiffness = 0.5
epsilon = 1e-06

SUB = 8
LANES = 128
LAPS = 3
FIELD = LAPS * RELAX
REACH = FIELD + 2
CHUNKS = (5, 4, 2)

VMEM = pl.BlockSpec(memory_space=pltpu.VMEM)
PARAMS = pltpu.CompilerParams(vmem_limit_bytes=8 << 20)


def neighbours(ref, i):
    c = ref[i]
    up = jnp.concatenate([c[1:], pltpu.roll(c[:1], SUB - 1, 1)], axis=0)
    down = jnp.concatenate([pltpu.roll(c[-1:], 1, 1), c[:-1]], axis=0)
    nz = c.shape[-1]
    side = pltpu.roll(c, 1, 2) + pltpu.roll(c, nz - 1, 2)
    return (ref[i - 1] + ref[i + 1]) + (up + down) + side - 6.0 * c


def potential_row(v, w, d):
    h2 = spacing * spacing
    return v * ((1.0 + undercool) + v * v) + (2.0 / h2) * w + (1.0 / (h2 * h2)) * d


def context(m):
    return LAPS if m % LAPS == 0 else 2


def level_row(levels, m, y):
    below, off = levels[m - 1]
    d = neighbours(below, y + off)
    kind = m % LAPS
    if kind == 1:
        return d
    w = below[y + off]
    ref, off = levels[m - 2 if kind == 2 else m - LAPS]
    v = ref[y + off]
    if kind == 2:
        return potential_row(v, w, d)
    return v + (time_step / (spacing * spacing)) * d


def rows_of(levels, m, start, stop, into):
    for i in range(stop[0] - start[0]):
        for side in range(2):
            ref, off = into[side]
            y = start[side] + i
            ref[y + off] = level_row(levels[side], m, y)


def cut_kernel(whole_ref, half_ref, sems):
    lanes = half_ref.shape[-1]
    copies = []
    for z in range(half_ref.shape[0]):
        part = whole_ref.at[1 - lax.axis_index("gx"), :, :, pl.ds(z * lanes, lanes)]
        copies.append(pltpu.make_async_copy(part, half_ref.at[z], sems.at[z]))
        copies[-1].start()
    for copy in copies:
        copy.wait()


def own_kernel(whole_ref, slab_ref, half_ref, sems):
    tiles, half, rows, lanes = half_ref.shape
    planes = slab_ref.shape[1]
    copies = []
    for z in range(tiles):
        part = whole_ref.at[lax.axis_index("gx"), :, :, pl.ds(z * lanes, lanes)]
        copies.append(pltpu.make_async_copy(part, half_ref.at[z], sems.at[z]))
        copies[-1].start()
    for copy in copies:
        copy.wait()
    flat = half_ref.reshape(tiles, half * rows, lanes)
    h = SUB // 2

    def body(y, carry):
        for r in range(planes):
            where = pl.ds(r * rows + y, h, stride=planes * rows)
            for z in range(tiles):
                slab_ref[y, r, :h, z * lanes : (z + 1) * lanes] = flat[z, where, :]
        return carry

    lax.fori_loop(0, rows, body, 0)


def first_kernel(rows, sends, own_ref, recv_ref, *refs):
    slab_ref, pieces = refs[0], refs[1:]
    tiles, half, _, lanes = recv_ref.shape
    planes = slab_ref.shape[1]
    flat = recv_ref.reshape(tiles, half * rows, lanes)
    h = SUB // 2

    def row(y):
        for r in range(planes):
            where = pl.ds(r * rows + y, h, stride=planes * rows)
            for z in range(tiles):
                at = slice(z * lanes, (z + 1) * lanes)
                value = jnp.concatenate([own_ref[y, r, :h, at], flat[z, where, :]], axis=0)
                slab_ref[y, r, :, at] = value
                yield r, at, value

    def plain(y, carry):
        for _ in row(y):
            pass
        return carry

    done = 0
    for start, count, piece in sorted(((*send, piece) for send, piece in zip(sends, pieces)), key=lambda s: s[0]):
        if start > done:
            lax.fori_loop(done, start, plain, 0)

        def body(i, carry, start=start, piece=piece):
            for r, at, value in row(start + i):
                piece[i, r, :, at] = value
            return carry

        lax.fori_loop(0, count, body, 0)
        done = start + count
    if rows > done:
        lax.fori_loop(done, rows, plain, 0)


def inner_kernel(rows, slab_ref, *outs):
    levels = [(slab_ref, 0)] + [(ref, -m) for m, ref in enumerate(outs, 1)]
    for m in range(1, FIELD + 1):
        count = (rows - 2 * m) // 2
        start, stop = (m, m + count), (m + count, rows - m)
        rows_of((levels, levels), m, start, stop, (levels[m], levels[m]))


def edge_kernel(rows, before, after, low_ref, high_ref, *refs):
    count = after - before
    past, levels = refs[:FIELD], refs[-FIELD:]
    fields = refs[FIELD:-FIELD]
    sides = ([], [])
    for m, (old, new) in enumerate(zip(past, levels)):
        c = context(m)
        total = count + c
        for i in range(c):
            new[count + i] = old[i]
            new[total + i] = old[old.shape[0] - c + i]
        sides[0].append((new, after - m))
        sides[1].append((new, total + c - (rows - m + before)))

    def fill(i, carry):
        levels[0][i] = low_ref[i]
        levels[0][count + 2 * context(0) + i] = high_ref[i]
        return carry

    lax.fori_loop(0, count, fill, 0)
    for m in range(1, FIELD):
        start = (m - after, rows - m + before)
        stop = (m - before, rows - m + after)
        rows_of(sides, m, start, stop, (sides[0][m], sides[1][m]))
    beyond = max(0, after - FIELD)
    kept = count - beyond
    if kept:
        low = FIELD - after + beyond
        high = rows - FIELD + before
        into = ((fields[0], -low), (fields[0], kept - high))
        rows_of(sides, FIELD, (low, high), (low + kept, high + kept), into)
    if beyond:
        into = ((fields[-1], beyond), (fields[-1], beyond - rows))
        rows_of(sides, FIELD, (-beyond, rows), (0, rows + beyond), into)


def keeping(gx):
    image = 2 * lax.axis_index("chain") + gx
    return jnp.logical_or(image == 0, image == 2 * lax.axis_size("chain") - 1)


def chemical_kernel(rows, segments, halo_ref, *refs):
    n = len(segments)
    pieces, outs = refs[:n], refs[n : 2 * n]
    field_ref, w_ref = refs[2 * n :]
    for i in range(2):
        field_ref[i] = halo_ref[i]
        field_ref[rows + 2 + i] = halo_ref[2 + i]
    for parts, piece in zip(segments, pieces):
        for start, count, first in parts:
            for i in range(count):
                field_ref[2 + start + i] = piece[first + i]
    for i in range(rows + 2):
        w_ref[i] = neighbours(field_ref, i + 1)
    for parts, out in zip(segments, outs):
        for start, count, first in parts:
            for i in range(count):
                y = start + i
                out[first + i] = potential_row(field_ref[y + 2], w_ref[y + 1], neighbours(w_ref, y + 1))


def sums_kernel(n, lanes, before_ref, *refs):
    sums_ref, outs = refs[4 * n], refs[4 * n + 1 :]
    keep = keeping(lax.axis_index("gx"))
    planes, nz = refs[0].shape[1], refs[0].shape[3]

    def fold(a):
        return sum(a[r, :, z : z + lanes] for r in range(planes) for z in range(0, nz, lanes))

    low = lax.broadcasted_iota(jnp.int32, (planes, SUB, nz), 1) < SUB // 2
    totals = [before_ref[q] for q in range(4)] if before_ref is not None else [jnp.zeros((SUB, lanes), jnp.float32)] * 4
    for j in range(n):
        piece, partner, chain, chemical = refs[j : 4 * n : n]
        mine, send = outs[2 * j], outs[2 * j + 1]

        def body(i, totals, piece=piece, partner=partner, chain=chain, chemical=chemical, mine=mine, send=send):
            f, a, b, chem = piece[i], partner[i], chain[i], chemical[i]
            t = a - b
            fr = pltpu.roll(f, SUB // 2, 1)
            cr = pltpu.roll(chem, SUB // 2, 1)
            da, db = a - fr, b - fr
            g = jnp.where(keep, f, f - step_size * chem)
            mine[i] = jnp.where(low, g, t)
            send[i] = jnp.where(low, t, g)
            parts = (fold(t * t), fold(da * da), fold(db * db), fold(cr * t))
            return tuple(total + part for total, part in zip(totals, parts))

        totals = lax.fori_loop(0, piece.shape[0], body, tuple(totals))
    for q in range(4):
        sums_ref[q] = totals[q]


def last_kernel(cells, segments, mine_sums, other_sums, *refs):
    n = len(segments)
    out_ref, natural, sems = refs[2 * n :]
    _, half, rows, _ = out_ref.shape
    _, tiles, _, _, lanes = natural.shape
    flat = natural.reshape(2, tiles, half * rows, lanes)
    planes = 2 * half // SUB
    h = SUB // 2

    gx = lax.axis_index("gx")
    images = (gx, 1 - gx)

    def factor(i):
        sums_ref = (mine_sums, other_sums)[i]

        def total(q):
            return jnp.sum(sums_ref[q], keepdims=True) / cells

        scale = lax.rsqrt(total(0) + epsilon)
        spring = stiffness * (jnp.sqrt(total(1) + epsilon) - jnp.sqrt(total(2) + epsilon))
        k = step_size * total(3) * scale * scale + spring * scale
        return jnp.where(keeping(images[i]), jnp.zeros_like(k), k)

    copies = []
    for i in range(2):
        k = factor(i)
        image = images[i]
        for parts, ref in zip(segments, refs[i * n : (i + 1) * n]):
            for start, count, first in parts:
                def body(j, carry, start=start, first=first, ref=ref, i=i, k=k):
                    for r in range(planes):
                        for z in range(tiles):
                            at = slice(z * lanes, (z + 1) * lanes)
                            v = ref[first + j, r, :, at]
                            v = v + k * pltpu.roll(v, h, 0)
                            where = pl.ds(r * rows + start + j, h, stride=planes * rows)
                            flat[i, z, where, :] = v[i * h : i * h + h]
                    return carry

                lax.fori_loop(0, count, body, 0)
        for z in range(tiles):
            part = out_ref.at[image, :, :, pl.ds(z * lanes, lanes)]
            copies.append(pltpu.make_async_copy(natural.at[i, z], part, sems.at[i, z]))
            copies[-1].start()
    for copy in copies:
        copy.wait()


def ring(axis, distance):
    n = lax.axis_size(axis)
    return [(i, (i + distance) % n) for i in range(n)]


def add_kernel(a_ref, b_ref, out_ref):
    out_ref[...] = a_ref[...] + b_ref[...]


def add(a, b):
    return pl.pallas_call(
        add_kernel,
        out_shape=jax.ShapeDtypeStruct(a.shape, a.dtype),
        in_specs=[VMEM] * 2,
        out_specs=VMEM,
        compiler_params=PARAMS,
        name="add",
    )(a, b)


def total_over(value, axis):
    n = lax.axis_size(axis)
    if n & (n - 1):
        others = [lax.ppermute(value, axis, ring(axis, d)) for d in range(1, n)]
        return functools.reduce(add, others, value)
    d = 1
    while d < n:
        value = add(value, lax.ppermute(value, axis, [(i, i ^ d) for i in range(n)]))
        d *= 2
    return value


def per_device(initial_path):
    count, half, rows, nz = initial_path.shape
    assert count == lax.axis_size("gx") == 2
    assert rows % 2 == 0 and rows >= 2 * REACH and half % SUB == 0 and nz % LANES == 0
    planes = 2 * half // SUB
    cells = 2 * half * rows * lax.axis_size("gy") * nz
    chains = lax.axis_size("chain")
    swap = [(0, 1), (1, 0)]
    tiles = nz // LANES
    hbm = pl.BlockSpec(memory_space=pl.ANY)

    def slab(n):
        return jax.ShapeDtypeStruct((n, planes, SUB, nz), jnp.float32)

    part = (tiles, half, rows, LANES)
    other = pl.pallas_call(
        cut_kernel,
        out_shape=jax.ShapeDtypeStruct(part, jnp.float32),
        in_specs=[hbm],
        out_specs=VMEM,
        scratch_shapes=[pltpu.SemaphoreType.DMA((tiles,))],
        compiler_params=PARAMS,
        name="cut",
    )(initial_path)
    recv = lax.ppermute(other, "gx", swap)
    own = pl.pallas_call(
        own_kernel,
        out_shape=slab(rows),
        in_specs=[hbm],
        out_specs=VMEM,
        scratch_shapes=[pltpu.VMEM(part, jnp.float32), pltpu.SemaphoreType.DMA((tiles,))],
        compiler_params=PARAMS,
        name="own",
    )(initial_path)
    known = [0]
    for n in CHUNKS:
        known.append(known[-1] + n)
    sends = []
    for a, b in zip(known, known[1:]):
        sends += [(a, b - a), (rows - b, b - a)]
    first = pl.pallas_call(
        functools.partial(first_kernel, rows, sends),
        out_shape=[slab(rows)] + [slab(n) for _, n in sends],
        in_specs=[VMEM] * 2,
        out_specs=[VMEM] * (1 + len(sends)),
        compiler_params=PARAMS,
        name="first",
    )(own, recv)
    halos = []
    for j in range(len(CHUNKS)):
        low, high = first[1 + 2 * j], first[2 + 2 * j]
        halos.append((
            lax.ppermute(high, "gy", ring("gy", 1)),
            lax.ppermute(low, "gy", ring("gy", -1)),
        ))

    inner = pl.pallas_call(
        functools.partial(inner_kernel, rows),
        out_shape=[slab(rows - 2 * m) for m in range(1, FIELD + 1)],
        in_specs=[VMEM],
        out_specs=[VMEM] * FIELD,
        compiler_params=PARAMS,
        name="inner",
    )(first[0])
    levels = [first[0]] + list(inner[:-1])
    pieces = [inner[-1]]
    segments = [[(FIELD, rows - 2 * FIELD, 0)]]
    for (low, high), a, b in zip(halos, known, known[1:]):
        beyond = max(0, b - FIELD)
        kept = b - a - beyond
        fields = [slab(2 * n) for n in (kept, beyond) if n]
        buffers = [(2 * (b - a + context(m)), planes, SUB, nz) for m in range(FIELD)]
        last = b == REACH
        outs = fields if last else fields + [slab(shape[0]) for shape in buffers]
        done = pl.pallas_call(
            functools.partial(edge_kernel, rows, a, b),
            out_shape=outs,
            in_specs=[VMEM] * (FIELD + 2),
            out_specs=[VMEM] * len(outs),
            scratch_shapes=[pltpu.VMEM(shape, jnp.float32) for shape in buffers] if last else [],
            compiler_params=PARAMS,
            name="edge",
        )(low, high, *levels)
        if kept:
            pieces.append(done[0])
            segments.append([(FIELD - a - kept, kept, 0), (rows - FIELD + a, kept, kept)])
        levels = list(done[len(fields) :])
        halo = done[len(fields) - 1]

    along_chain = []
    for c in range(chains - 1):
        along_chain += [(2 * c + 1, 2 * c + 2), (2 * c + 2, 2 * c + 1)]
    from_partner = [lax.ppermute(p, "gx", swap) for p in pieces]
    from_chain = [lax.ppermute(p, ("chain", "gx"), along_chain) for p in pieces]

    chemical = pl.pallas_call(
        functools.partial(chemical_kernel, rows, segments),
        out_shape=[slab(p.shape[0]) for p in pieces],
        in_specs=[VMEM] * (1 + len(pieces)),
        out_specs=[VMEM] * len(pieces),
        scratch_shapes=[
            pltpu.VMEM((rows + 4, planes, SUB, nz), jnp.float32),
            pltpu.VMEM((rows + 2, planes, SUB, nz), jnp.float32),
        ],
        compiler_params=PARAMS,
        name="chemical",
    )(halo, *pieces)
    mine, halfway, total = [], [], None
    for some in (slice(0, -1), slice(-1, None)):
        n = len(pieces[some])
        before = [] if total is None else [total]
        kernel = functools.partial(sums_kernel, n, LANES)
        total, *outs = pl.pallas_call(
            kernel if before else functools.partial(kernel, None),
            out_shape=[jax.ShapeDtypeStruct((4, SUB, LANES), jnp.float32)]
            + [slab(p.shape[0]) for p in pieces[some] for _ in range(2)],
            in_specs=[VMEM] * (4 * n + len(before)),
            out_specs=[VMEM] * (1 + 2 * n),
            compiler_params=PARAMS,
            name="sums",
        )(*before, *pieces[some], *from_partner[some], *from_chain[some], *chemical[some])
        mine += outs[::2]
        halfway += [lax.ppermute(send, "gx", swap) for send in outs[1::2]]
    total = total_over(total, "gy")
    other = lax.ppermute(total, "gx", swap)
    return pl.pallas_call(
        functools.partial(last_kernel, cells, segments),
        out_shape=jax.ShapeDtypeStruct(initial_path.shape, jnp.float32),
        in_specs=[VMEM] * (2 + 2 * len(pieces)),
        out_specs=hbm,
        scratch_shapes=[
            pltpu.VMEM((2, *part), jnp.float32),
            pltpu.SemaphoreType.DMA((2, tiles)),
        ],
        compiler_params=PARAMS,
        name="last",
    )(total, other, *mine, *halfway)


def solution(mesh):
    return jax.shard_map(
        per_device,
        mesh=mesh,
        in_specs=(P("chain", "gx", "gy", None),),
        out_specs=P("chain", "gx", "gy", None),
        check_vma=False,
    )
```

```python
import functools

import jax
import jax.numpy as jnp
from jax import lax
from jax.experimental import pallas as pl
from jax.experimental.pallas import tpu as pltpu
from jax.sharding import PartitionSpec as P

RELAX = 3

spacing = 0.7853981633974483
undercool = -0.25
time_step = 0.00025
step_size = 0.002
stiffness = 0.5
epsilon = 1e-06

SUB = 8
LANES = 128
LAPS = 3
FIELD = LAPS * RELAX
REACH = FIELD + 2
LEAD = 2
CHUNKS = (4, 3, 2, 2)

VMEM = pl.BlockSpec(memory_space=pltpu.VMEM)
SCALE = 1.0


def cost(rows):
    return pl.CostEstimate(flops=0, bytes_accessed=int(SCALE * 130000 * rows), transcendentals=0)


PARAMS = pltpu.CompilerParams(vmem_limit_bytes=8 << 20)


def neighbours(ref, i):
    c = ref[i]
    up = jnp.concatenate([c[1:], pltpu.roll(c[:1], SUB - 1, 1)], axis=0)
    down = jnp.concatenate([pltpu.roll(c[-1:], 1, 1), c[:-1]], axis=0)
    nz = c.shape[-1]
    side = pltpu.roll(c, 1, 2) + pltpu.roll(c, nz - 1, 2)
    return (ref[i - 1] + ref[i + 1]) + (up + down) + side - 6.0 * c


def potential_row(v, w, d):
    h2 = spacing * spacing
    return v * ((1.0 + undercool) + v * v) + (2.0 / h2) * w + (1.0 / (h2 * h2)) * d


def context(m):
    return LAPS if m % LAPS == 0 else 2


def level_row(levels, m, y):
    below, off = levels[m - 1]
    d = neighbours(below, y + off)
    kind = m % LAPS
    if kind == 1:
        return d
    w = below[y + off]
    ref, off = levels[m - 2 if kind == 2 else m - LAPS]
    v = ref[y + off]
    if kind == 2:
        return potential_row(v, w, d)
    return v + (time_step / (spacing * spacing)) * d


def rows_of(levels, m, start, stop, into):
    for i in range(stop[0] - start[0]):
        for side in range(2):
            ref, off = into[side]
            y = start[side] + i
            ref[y + off] = level_row(levels[side], m, y)


def cut_kernel(whole_ref, half_ref, sems):
    lanes = half_ref.shape[-1]
    copies = []
    for z in range(half_ref.shape[0]):
        part = whole_ref.at[1 - lax.axis_index("gx"), :, :, pl.ds(z * lanes, lanes)]
        copies.append(pltpu.make_async_copy(part, half_ref.at[z], sems.at[z]))
        copies[-1].start()
    for copy in copies:
        copy.wait()


def own_kernel(whole_ref, slab_ref, half_ref, sems):
    tiles, half, rows, lanes = half_ref.shape
    planes = slab_ref.shape[1]
    copies = []
    for z in range(tiles):
        part = whole_ref.at[lax.axis_index("gx"), :, :, pl.ds(z * lanes, lanes)]
        copies.append(pltpu.make_async_copy(part, half_ref.at[z], sems.at[z]))
        copies[-1].start()
    for copy in copies:
        copy.wait()
    flat = half_ref.reshape(tiles, half * rows, lanes)
    h = SUB // 2

    def body(y, carry):
        for r in range(planes):
            where = pl.ds(r * rows + y, h, stride=planes * rows)
            for z in range(tiles):
                slab_ref[y, r, :h, z * lanes : (z + 1) * lanes] = flat[z, where, :]
        return carry

    lax.fori_loop(0, rows, body, 0)


def first_kernel(rows, sends, own_ref, recv_ref, *refs):
    slab_ref, pieces = refs[0], refs[1:]
    tiles, half, _, lanes = recv_ref.shape
    planes = slab_ref.shape[1]
    flat = recv_ref.reshape(tiles, half * rows, lanes)
    h = SUB // 2

    def row(y):
        for r in range(planes):
            where = pl.ds(r * rows + y, h, stride=planes * rows)
            for z in range(tiles):
                at = slice(z * lanes, (z + 1) * lanes)
                value = jnp.concatenate([own_ref[y, r, :h, at], flat[z, where, :]], axis=0)
                slab_ref[y, r, :, at] = value
                yield r, at, value

    def plain(y, carry):
        for _ in row(y):
            pass
        return carry

    done = 0
    for start, count, piece in sorted(((*send, piece) for send, piece in zip(sends, pieces)), key=lambda s: s[0]):
        if start > done:
            lax.fori_loop(done, start, plain, 0)

        def body(i, carry, start=start, piece=piece):
            for r, at, value in row(start + i):
                piece[i, r, :, at] = value
            return carry

        lax.fori_loop(0, count, body, 0)
        done = start + count
    if rows > done:
        lax.fori_loop(done, rows, plain, 0)


def send_rows(sends, slab_ref, pieces):
    for piece, (start, count) in zip(pieces, sends):
        for i in range(count):
            piece[i] = slab_ref[start + i]


def inner_kernel(rows, sends, slab_ref, *refs):
    outs = refs[:FIELD]
    send_rows(sends, slab_ref, refs[FIELD:])
    levels = [(slab_ref, 0)] + [(ref, -m) for m, ref in enumerate(outs, 1)]
    for m in range(1, FIELD + 1):
        count = (rows - 2 * m) // 2
        start, stop = (m, m + count), (m + count, rows - m)
        rows_of((levels, levels), m, start, stop, (levels[m], levels[m]))


def edge_kernel(rows, before, after, sends, early, slab_ref, low_ref, high_ref, *refs):
    count = after - before
    n = len(sends)
    refs = refs[:FIELD] + refs[FIELD + early :]
    send_rows(sends, slab_ref, refs[FIELD : FIELD + n])
    refs = refs[:FIELD] + refs[FIELD + n :]
    past, levels = refs[:FIELD], refs[-FIELD:]
    fields = refs[FIELD:-FIELD]
    sides = ([], [])
    for m, (old, new) in enumerate(zip(past, levels)):
        c = context(m)
        total = count + c
        for i in range(c):
            new[count + i] = old[i]
            new[total + i] = old[old.shape[0] - c + i]
        sides[0].append((new, after - m))
        sides[1].append((new, total + c - (rows - m + before)))

    def fill(i, carry):
        levels[0][i] = low_ref[i]
        levels[0][count + 2 * context(0) + i] = high_ref[i]
        return carry

    lax.fori_loop(0, count, fill, 0)
    for m in range(1, FIELD):
        start = (m - after, rows - m + before)
        stop = (m - before, rows - m + after)
        rows_of(sides, m, start, stop, (sides[0][m], sides[1][m]))
    beyond = max(0, after - FIELD)
    kept = count - beyond
    if kept:
        low = FIELD - after + beyond
        high = rows - FIELD + before
        into = ((fields[0], -low), (fields[0], kept - high))
        rows_of(sides, FIELD, (low, high), (low + kept, high + kept), into)
    if beyond:
        into = ((fields[-1], beyond), (fields[-1], beyond - rows))
        rows_of(sides, FIELD, (-beyond, rows), (0, rows + beyond), into)


def keeping(gx):
    image = 2 * lax.axis_index("chain") + gx
    return jnp.logical_or(image == 0, image == 2 * lax.axis_size("chain") - 1)


def chemical_kernel(rows, segments, halo_ref, *refs):
    n = len(segments)
    pieces, outs = refs[:n], refs[n : 2 * n]
    field_ref, w_ref = refs[2 * n :]
    for i in range(2):
        field_ref[i] = halo_ref[i]
        field_ref[rows + 2 + i] = halo_ref[2 + i]
    for parts, piece in zip(segments, pieces):
        for start, count, first in parts:
            for i in range(count):
                field_ref[2 + start + i] = piece[first + i]
    for i in range(rows + 2):
        w_ref[i] = neighbours(field_ref, i + 1)
    for parts, out in zip(segments, outs):
        for start, count, first in parts:
            for i in range(count):
                y = start + i
                out[first + i] = potential_row(field_ref[y + 2], w_ref[y + 1], neighbours(w_ref, y + 1))


def sums_kernel(n, lanes, before_ref, *refs):
    sums_ref, outs = refs[4 * n], refs[4 * n + 1 :]
    keep = keeping(lax.axis_index("gx"))
    planes, nz = refs[0].shape[1], refs[0].shape[3]

    def fold(a):
        return sum(a[r, :, z : z + lanes] for r in range(planes) for z in range(0, nz, lanes))

    low = lax.broadcasted_iota(jnp.int32, (planes, SUB, nz), 1) < SUB // 2
    totals = [before_ref[q] for q in range(4)] if before_ref is not None else [jnp.zeros((SUB, lanes), jnp.float32)] * 4
    for j in range(n):
        piece, partner, chain, chemical = refs[j : 4 * n : n]
        mine, send = outs[2 * j], outs[2 * j + 1]

        def body(i, totals, piece=piece, partner=partner, chain=chain, chemical=chemical, mine=mine, send=send):
            f, a, b, chem = piece[i], partner[i], chain[i], chemical[i]
            t = a - b
            fr = pltpu.roll(f, SUB // 2, 1)
            cr = pltpu.roll(chem, SUB // 2, 1)
            da, db = a - fr, b - fr
            g = jnp.where(keep, f, f - step_size * chem)
            mine[i] = jnp.where(low, g, t)
            send[i] = jnp.where(low, t, g)
            parts = (fold(t * t), fold(da * da), fold(db * db), fold(cr * t))
            return tuple(total + part for total, part in zip(totals, parts))

        totals = lax.fori_loop(0, piece.shape[0], body, tuple(totals))
    for q in range(4):
        sums_ref[q] = totals[q]


def last_kernel(cells, segments, mine_sums, other_sums, *refs):
    n = len(segments)
    out_ref, natural, sems = refs[2 * n :]
    _, half, rows, _ = out_ref.shape
    _, tiles, _, _, lanes = natural.shape
    flat = natural.reshape(2, tiles, half * rows, lanes)
    planes = 2 * half // SUB
    h = SUB // 2

    gx = lax.axis_index("gx")
    images = (gx, 1 - gx)

    def factor(i):
        sums_ref = (mine_sums, other_sums)[i]

        def total(q):
            return jnp.sum(sums_ref[q], keepdims=True) / cells

        scale = lax.rsqrt(total(0) + epsilon)
        spring = stiffness * (jnp.sqrt(total(1) + epsilon) - jnp.sqrt(total(2) + epsilon))
        k = step_size * total(3) * scale * scale + spring * scale
        return jnp.where(keeping(images[i]), jnp.zeros_like(k), k)

    copies = []
    for i in range(2):
        k = factor(i)
        image = images[i]
        for parts, ref in zip(segments, refs[i * n : (i + 1) * n]):
            for start, count, first in parts:
                def body(j, carry, start=start, first=first, ref=ref, i=i, k=k):
                    for r in range(planes):
                        for z in range(tiles):
                            at = slice(z * lanes, (z + 1) * lanes)
                            v = ref[first + j, r, :, at]
                            v = v + k * pltpu.roll(v, h, 0)
                            where = pl.ds(r * rows + start + j, h, stride=planes * rows)
                            flat[i, z, where, :] = v[i * h : i * h + h]
                    return carry

                lax.fori_loop(0, count, body, 0)
        for z in range(tiles):
            part = out_ref.at[image, :, :, pl.ds(z * lanes, lanes)]
            copies.append(pltpu.make_async_copy(natural.at[i, z], part, sems.at[i, z]))
            copies[-1].start()
    for copy in copies:
        copy.wait()


def ring(axis, distance):
    n = lax.axis_size(axis)
    return [(i, (i + distance) % n) for i in range(n)]


def add_kernel(a_ref, b_ref, out_ref):
    out_ref[...] = a_ref[...] + b_ref[...]


def add(a, b):
    return pl.pallas_call(
        add_kernel,
        out_shape=jax.ShapeDtypeStruct(a.shape, a.dtype),
        in_specs=[VMEM] * 2,
        out_specs=VMEM,
        compiler_params=PARAMS,
        cost_estimate=cost(1),
        name="add",
    )(a, b)


def total_over(value, axis):
    n = lax.axis_size(axis)
    if n & (n - 1):
        others = [lax.ppermute(value, axis, ring(axis, d)) for d in range(1, n)]
        return functools.reduce(add, others, value)
    d = 1
    while d < n:
        value = add(value, lax.ppermute(value, axis, [(i, i ^ d) for i in range(n)]))
        d *= 2
    return value


def per_device(initial_path):
    count, half, rows, nz = initial_path.shape
    assert count == lax.axis_size("gx") == 2
    assert rows % 2 == 0 and rows >= 2 * REACH and half % SUB == 0 and nz % LANES == 0
    planes = 2 * half // SUB
    cells = 2 * half * rows * lax.axis_size("gy") * nz
    chains = lax.axis_size("chain")
    swap = [(0, 1), (1, 0)]
    tiles = nz // LANES
    hbm = pl.BlockSpec(memory_space=pl.ANY)

    def slab(n):
        return jax.ShapeDtypeStruct((n, planes, SUB, nz), jnp.float32)

    part = (tiles, half, rows, LANES)
    other = pl.pallas_call(
        cut_kernel,
        out_shape=jax.ShapeDtypeStruct(part, jnp.float32),
        in_specs=[hbm],
        out_specs=VMEM,
        scratch_shapes=[pltpu.SemaphoreType.DMA((tiles,))],
        compiler_params=PARAMS,
        cost_estimate=cost(4),
        name="cut",
    )(initial_path)
    recv = lax.ppermute(other, "gx", swap)
    own = pl.pallas_call(
        own_kernel,
        out_shape=slab(rows),
        in_specs=[hbm],
        out_specs=VMEM,
        scratch_shapes=[pltpu.VMEM(part, jnp.float32), pltpu.SemaphoreType.DMA((tiles,))],
        compiler_params=PARAMS,
        cost_estimate=cost(18),
        name="own",
    )(initial_path)
    known = [0]
    for n in CHUNKS:
        known.append(known[-1] + n)
    sends = [[(a, b - a), (rows - b, b - a)] for a, b in zip(known, known[1:])]
    made = [[], [], []] + [[] for _ in CHUNKS]
    for j, some in enumerate(sends):
        made[max(0, j - LEAD)] += some
    whole, *near = pl.pallas_call(
        functools.partial(first_kernel, rows, made[0]),
        out_shape=[slab(rows)] + [slab(n) for _, n in made[0]],
        in_specs=[VMEM] * 2,
        out_specs=[VMEM] * (1 + len(made[0])),
        compiler_params=PARAMS,
        cost_estimate=cost(18),
        name="first",
    )(own, recv)
    along_chain = []
    for c in range(chains - 1):
        along_chain += [(2 * c + 1, 2 * c + 2), (2 * c + 2, 2 * c + 1)]
    from_partner, from_chain = [], []

    def exchange(piece):
        from_chain.append(lax.ppermute(piece, ("chain", "gx"), along_chain))
        from_partner.append(lax.ppermute(piece, "gx", swap))

    def halos_of(edges):
        for low, high in zip(edges[::2], edges[1::2]):
            halos.append((
                lax.ppermute(high, "gy", ring("gy", 1)),
                lax.ppermute(low, "gy", ring("gy", -1)),
            ))

    halos = []
    halos_of(near)
    inner = pl.pallas_call(
        functools.partial(inner_kernel, rows, made[1]),
        out_shape=[slab(rows - 2 * m) for m in range(1, FIELD + 1)] + [slab(n) for _, n in made[1]],
        in_specs=[VMEM],
        out_specs=[VMEM] * (FIELD + len(made[1])),
        compiler_params=PARAMS,
        cost_estimate=cost(126),
        name="inner",
    )(whole)
    levels = [whole] + list(inner[: FIELD - 1])
    halos_of(inner[FIELD:])
    pieces = [inner[FIELD - 1]]
    exchange(pieces[0])
    segments = [[(FIELD, rows - 2 * FIELD, 0)]]
    for j, (a, b) in enumerate(zip(known, known[1:])):
        beyond = max(0, b - FIELD)
        kept = b - a - beyond
        fields = [slab(2 * n) for n in (kept, beyond) if n]
        buffers = [(2 * (b - a + context(m)), planes, SUB, nz) for m in range(FIELD)]
        last = b == REACH
        ahead = made[j + 2]
        outs = [slab(n) for _, n in ahead] + fields
        if not last:
            outs += [slab(shape[0]) for shape in buffers]
        early = from_chain[j - 1 : j] if j else []
        done = pl.pallas_call(
            functools.partial(edge_kernel, rows, a, b, ahead, len(early)),
            out_shape=outs,
            in_specs=[VMEM] * (FIELD + 3 + len(early)),
            out_specs=[VMEM] * len(outs),
            scratch_shapes=[pltpu.VMEM(shape, jnp.float32) for shape in buffers] if last else [],
            compiler_params=PARAMS,
            cost_estimate=cost(2 * FIELD * (b - a)),
            name="edge",
        )(whole, *halos[j], *levels, *early)
        halos_of(done[: len(ahead)])
        done = done[len(ahead) :]
        if kept:
            pieces.append(done[0])
            exchange(done[0])
            segments.append([(FIELD - a - kept, kept, 0), (rows - FIELD + a, kept, kept)])
        levels = list(done[len(fields) :])
        beyond_rows = done[len(fields) - 1]

    chemical = pl.pallas_call(
        functools.partial(chemical_kernel, rows, segments),
        out_shape=[slab(p.shape[0]) for p in pieces],
        in_specs=[VMEM] * (1 + len(pieces)),
        out_specs=[VMEM] * len(pieces),
        scratch_shapes=[
            pltpu.VMEM((rows + 4, planes, SUB, nz), jnp.float32),
            pltpu.VMEM((rows + 2, planes, SUB, nz), jnp.float32),
        ],
        compiler_params=PARAMS,
        cost_estimate=cost(2 * rows),
        name="chemical",
    )(beyond_rows, *pieces)
    mine, halfway, total = [], [], None
    for some in (slice(0, -1), slice(-1, None)):
        n = len(pieces[some])
        before = [] if total is None else [total]
        kernel = functools.partial(sums_kernel, n, LANES)
        total, *outs = pl.pallas_call(
            kernel if before else functools.partial(kernel, None),
            out_shape=[jax.ShapeDtypeStruct((4, SUB, LANES), jnp.float32)]
            + [slab(p.shape[0]) for p in pieces[some] for _ in range(2)],
            in_specs=[VMEM] * (4 * n + len(before)),
            out_specs=[VMEM] * (1 + 2 * n),
            compiler_params=PARAMS,
            cost_estimate=cost(rows // 2),
            name="sums",
        )(*before, *pieces[some], *from_partner[some], *from_chain[some], *chemical[some])
        mine += outs[::2]
        halfway += [lax.ppermute(send, "gx", swap) for send in outs[1::2]]
    total = total_over(total, "gy")
    other = lax.ppermute(total, "gx", swap)
    return pl.pallas_call(
        functools.partial(last_kernel, cells, segments),
        out_shape=jax.ShapeDtypeStruct(initial_path.shape, jnp.float32),
        in_specs=[VMEM] * (2 + 2 * len(pieces)),
        out_specs=hbm,
        scratch_shapes=[
            pltpu.VMEM((2, *part), jnp.float32),
            pltpu.SemaphoreType.DMA((2, tiles)),
        ],
        compiler_params=PARAMS,
        cost_estimate=cost(2 * rows),
        name="last",
    )(total, other, *mine, *halfway)


def solution(mesh):
    return jax.shard_map(
        per_device,
        mesh=mesh,
        in_specs=(P("chain", "gx", "gy", None),),
        out_specs=P("chain", "gx", "gy", None),
        check_vma=False,
    )
```

```python
import functools

import jax
import jax.numpy as jnp
from jax import lax
from jax.experimental import pallas as pl
from jax.experimental.pallas import tpu as pltpu
from jax.sharding import PartitionSpec as P

RELAX = 3

spacing = 0.7853981633974483
undercool = -0.25
time_step = 0.00025
step_size = 0.002
stiffness = 0.5
epsilon = 1e-06

SUB = 8
LANES = 128
BLOCKS = 4
LAPS = 3
FIELD = LAPS * RELAX
REACH = FIELD + 2
LEAD = 2
CHUNKS = (4, 3, 2, 2)

VMEM = pl.BlockSpec(memory_space=pltpu.VMEM)
SCALE = 1.0


def cost(rows):
    return pl.CostEstimate(flops=0, bytes_accessed=int(SCALE * 130000 * rows), transcendentals=0)


PARAMS = pltpu.CompilerParams(vmem_limit_bytes=8 << 20)


def neighbours(ref, i):
    c = ref[i]
    up = jnp.concatenate([c[1:], pltpu.roll(c[:1], SUB - 1, 1)], axis=0)
    down = jnp.concatenate([pltpu.roll(c[-1:], 1, 1), c[:-1]], axis=0)
    nz = c.shape[-1]
    side = pltpu.roll(c, 1, 2) + pltpu.roll(c, nz - 1, 2)
    return (ref[i - 1] + ref[i + 1]) + (up + down) + side - 6.0 * c


def potential_row(v, w, d):
    h2 = spacing * spacing
    return v * ((1.0 + undercool) + v * v) + (2.0 / h2) * w + (1.0 / (h2 * h2)) * d


def context(m):
    return LAPS if m % LAPS == 0 else 2


def level_row(levels, m, y):
    below, off = levels[m - 1]
    d = neighbours(below, y + off)
    kind = m % LAPS
    if kind == 1:
        return d
    w = below[y + off]
    ref, off = levels[m - 2 if kind == 2 else m - LAPS]
    v = ref[y + off]
    if kind == 2:
        return potential_row(v, w, d)
    return v + (time_step / (spacing * spacing)) * d


def rows_of(levels, m, start, stop, into):
    for i in range(stop[0] - start[0]):
        for side in range(2):
            ref, off = into[side]
            y = start[side] + i
            ref[y + off] = level_row(levels[side], m, y)


def cut_kernel(whole_ref, half_ref, sems):
    lanes = half_ref.shape[-1]
    copies = []
    for z in range(half_ref.shape[0]):
        part = whole_ref.at[1 - lax.axis_index("gx"), :, :, pl.ds(z * lanes, lanes)]
        copies.append(pltpu.make_async_copy(part, half_ref.at[z], sems.at[z]))
        copies[-1].start()
    for copy in copies:
        copy.wait()


def own_kernel(whole_ref, slab_ref, half_ref, sems):
    tiles, half, rows, lanes = half_ref.shape
    planes = slab_ref.shape[1]
    copies = []
    for z in range(tiles):
        part = whole_ref.at[lax.axis_index("gx"), :, :, pl.ds(z * lanes, lanes)]
        copies.append(pltpu.make_async_copy(part, half_ref.at[z], sems.at[z]))
        copies[-1].start()
    for copy in copies:
        copy.wait()
    flat = half_ref.reshape(tiles, half * rows, lanes)
    h = SUB // 2

    def body(y, carry):
        for r in range(planes):
            where = pl.ds(r * rows + y, h, stride=planes * rows)
            for z in range(tiles):
                slab_ref[y, r, :h, z * lanes : (z + 1) * lanes] = flat[z, where, :]
        return carry

    lax.fori_loop(0, rows, body, 0)


def first_kernel(rows, sends, own_ref, recv_ref, *refs):
    slab_ref, pieces = refs[0], refs[1:]
    tiles, half, _, lanes = recv_ref.shape
    planes = slab_ref.shape[1]
    flat = recv_ref.reshape(tiles, half * rows, lanes)
    h = SUB // 2

    def row(y):
        for r in range(planes):
            where = pl.ds(r * rows + y, h, stride=planes * rows)
            for z in range(tiles):
                at = slice(z * lanes, (z + 1) * lanes)
                value = jnp.concatenate([own_ref[y, r, :h, at], flat[z, where, :]], axis=0)
                slab_ref[y, r, :, at] = value
                yield r, at, value

    def plain(y, carry):
        for _ in row(y):
            pass
        return carry

    done = 0
    for start, count, piece in sorted(((*send, piece) for send, piece in zip(sends, pieces)), key=lambda s: s[0]):
        if start > done:
            lax.fori_loop(done, start, plain, 0)

        def body(i, carry, start=start, piece=piece):
            for r, at, value in row(start + i):
                piece[i, r, :, at] = value
            return carry

        lax.fori_loop(0, count, body, 0)
        done = start + count
    if rows > done:
        lax.fori_loop(done, rows, plain, 0)


def send_rows(sends, slab_ref, pieces):
    for piece, (start, count) in zip(pieces, sends):
        for i in range(count):
            piece[i] = slab_ref[start + i]


def inner_kernel(rows, sends, slab_ref, *refs):
    outs = refs[:FIELD]
    send_rows(sends, slab_ref, refs[FIELD:])
    levels = [(slab_ref, 0)] + [(ref, -m) for m, ref in enumerate(outs, 1)]
    for m in range(1, FIELD + 1):
        count = (rows - 2 * m) // 2
        start, stop = (m, m + count), (m + count, rows - m)
        rows_of((levels, levels), m, start, stop, (levels[m], levels[m]))


def edge_kernel(rows, before, after, sends, early, slab_ref, low_ref, high_ref, *refs):
    count = after - before
    n = len(sends)
    refs = refs[:FIELD] + refs[FIELD + early :]
    send_rows(sends, slab_ref, refs[FIELD : FIELD + n])
    refs = refs[:FIELD] + refs[FIELD + n :]
    past, levels = refs[:FIELD], refs[-FIELD:]
    fields = refs[FIELD:-FIELD]
    sides = ([], [])
    for m, (old, new) in enumerate(zip(past, levels)):
        c = context(m)
        total = count + c
        for i in range(c):
            new[count + i] = old[i]
            new[total + i] = old[old.shape[0] - c + i]
        sides[0].append((new, after - m))
        sides[1].append((new, total + c - (rows - m + before)))

    def fill(i, carry):
        levels[0][i] = low_ref[i]
        levels[0][count + 2 * context(0) + i] = high_ref[i]
        return carry

    lax.fori_loop(0, count, fill, 0)
    for m in range(1, FIELD):
        start = (m - after, rows - m + before)
        stop = (m - before, rows - m + after)
        rows_of(sides, m, start, stop, (sides[0][m], sides[1][m]))
    beyond = max(0, after - FIELD)
    kept = count - beyond
    if kept:
        low = FIELD - after + beyond
        high = rows - FIELD + before
        into = ((fields[0], -low), (fields[0], kept - high))
        rows_of(sides, FIELD, (low, high), (low + kept, high + kept), into)
    if beyond:
        into = ((fields[-1], beyond), (fields[-1], beyond - rows))
        rows_of(sides, FIELD, (-beyond, rows), (0, rows + beyond), into)


def keeping(gx):
    image = 2 * lax.axis_index("chain") + gx
    return jnp.logical_or(image == 0, image == 2 * lax.axis_size("chain") - 1)


def chemical_kernel(rows, segments, halo_ref, *refs):
    n = len(segments)
    pieces, outs = refs[:n], refs[n : 2 * n]
    field_ref, w_ref = refs[2 * n :]
    for i in range(2):
        field_ref[i] = halo_ref[i]
        field_ref[rows + 2 + i] = halo_ref[2 + i]
    for parts, piece in zip(segments, pieces):
        for start, count, first in parts:
            for i in range(count):
                field_ref[2 + start + i] = piece[first + i]
    for i in range(rows + 2):
        w_ref[i] = neighbours(field_ref, i + 1)
    for parts, out in zip(segments, outs):
        for start, count, first in parts:
            for i in range(count):
                y = start + i
                out[first + i] = potential_row(field_ref[y + 2], w_ref[y + 1], neighbours(w_ref, y + 1))


def sums_kernel(n, lanes, before_ref, *refs):
    sums_ref, outs = refs[4 * n], refs[4 * n + 1 :]
    keep = keeping(lax.axis_index("gx"))
    planes, nz = refs[0].shape[1], refs[0].shape[3]

    def fold(a):
        return sum(a[r, :, z : z + lanes] for r in range(planes) for z in range(0, nz, lanes))

    low = lax.broadcasted_iota(jnp.int32, (planes, SUB, nz), 1) < SUB // 2
    totals = [before_ref[q] for q in range(4)] if before_ref is not None else [jnp.zeros((SUB, lanes), jnp.float32)] * 4
    for j in range(n):
        piece, partner, chain, chemical = refs[j : 4 * n : n]
        mine, send = outs[2 * j], outs[2 * j + 1]

        def body(i, totals, piece=piece, partner=partner, chain=chain, chemical=chemical, mine=mine, send=send):
            f, a, b, chem = piece[i], partner[i], chain[i], chemical[i]
            t = a - b
            fr = pltpu.roll(f, SUB // 2, 1)
            cr = pltpu.roll(chem, SUB // 2, 1)
            da, db = a - fr, b - fr
            g = jnp.where(keep, f, f - step_size * chem)
            mine[i] = jnp.where(low, g, t)
            send[i] = jnp.where(low, t, g)
            parts = (fold(t * t), fold(da * da), fold(db * db), fold(cr * t))
            return tuple(total + part for total, part in zip(totals, parts))

        totals = lax.fori_loop(0, piece.shape[0], body, tuple(totals))
    for q in range(4):
        sums_ref[q] = totals[q]


def layout_kernel(segments, low, *refs):
    n = len(segments)
    pair_ref, natural, sems = refs[n:]
    _, tiles, half, rows, lanes = natural.shape
    flat = natural.reshape(2, tiles, half * rows, lanes)
    planes = 2 * half // SUB
    h = SUB // 2
    for parts, ref in zip(segments, refs[:n]):
        for start, count, first in parts:
            def body(j, carry, start=start, first=first, ref=ref):
                for r in range(planes):
                    for z in range(tiles):
                        v = ref[first + j, r, :, z * lanes : (z + 1) * lanes]
                        where = pl.ds(r * rows + start + j, h, stride=planes * rows)
                        flat[0, z, where, :] = v[low : low + h]
                        flat[1, z, where, :] = v[h - low : 2 * h - low]
                return carry

            lax.fori_loop(0, count, body, 0)
    copies = []
    for i in range(2):
        for z in range(tiles):
            part = pair_ref.at[i, :, :, pl.ds(z * lanes, lanes)]
            copies.append(pltpu.make_async_copy(natural.at[i, z], part, sems.at[i, z]))
            copies[-1].start()
    for copy in copies:
        copy.wait()


def last_kernel(cells, own, sums_ref, pair_ref, *refs):
    out_ref, whole, sems = refs[-3:]
    half = whole.shape[0]
    gx = lax.axis_index("gx")
    image = gx if own else 1 - gx

    def total(q):
        return jnp.sum(sums_ref[q], keepdims=True) / cells

    scale = lax.rsqrt(total(0) + epsilon)
    spring = stiffness * (jnp.sqrt(total(1) + epsilon) - jnp.sqrt(total(2) + epsilon))
    k = step_size * total(3) * scale * scale + spring * scale
    k = jnp.where(keeping(image), jnp.zeros_like(k), k)
    copies = []
    step = half // BLOCKS
    for i in range(BLOCKS):
        block = pl.ds(i * step, step)
        whole[block] = pair_ref[0, block] + k * pair_ref[1, block]
        copies.append(pltpu.make_async_copy(whole.at[block], out_ref.at[image, block], sems.at[i]))
        copies[-1].start()
    for copy in copies:
        copy.wait()


def ring(axis, distance):
    n = lax.axis_size(axis)
    return [(i, (i + distance) % n) for i in range(n)]


def add_kernel(a_ref, b_ref, *refs):
    refs[-1][...] = a_ref[...] + b_ref[...]


def add(a, b, *beside):
    return pl.pallas_call(
        add_kernel,
        out_shape=jax.ShapeDtypeStruct(a.shape, a.dtype),
        in_specs=[VMEM] * (2 + len(beside)),
        out_specs=VMEM,
        compiler_params=PARAMS,
        cost_estimate=cost(1),
        name="add",
    )(a, b, *beside)


def total_over(value, axis, beside):
    n = lax.axis_size(axis)
    routes = [ring(axis, d) for d in range(1, n)]
    if n & (n - 1) == 0:
        routes = [[(i, i ^ d) for i in range(n)] for d in (1 << b for b in range(n.bit_length() - 1))]
    start = value
    for route in routes:
        last = route is routes[-1]
        moved = lax.ppermute(start if n & (n - 1) else value, axis, route)
        value = add(value, moved, *(beside if last else ()))
    return value


def per_device(initial_path):
    count, half, rows, nz = initial_path.shape
    assert count == lax.axis_size("gx") == 2
    assert rows % 2 == 0 and rows >= 2 * REACH and half % (SUB * BLOCKS) == 0 and nz % LANES == 0
    planes = 2 * half // SUB
    cells = 2 * half * rows * lax.axis_size("gy") * nz
    chains = lax.axis_size("chain")
    swap = [(0, 1), (1, 0)]
    tiles = nz // LANES
    hbm = pl.BlockSpec(memory_space=pl.ANY)

    def slab(n):
        return jax.ShapeDtypeStruct((n, planes, SUB, nz), jnp.float32)

    part = (tiles, half, rows, LANES)
    other = pl.pallas_call(
        cut_kernel,
        out_shape=jax.ShapeDtypeStruct(part, jnp.float32),
        in_specs=[hbm],
        out_specs=VMEM,
        scratch_shapes=[pltpu.SemaphoreType.DMA((tiles,))],
        compiler_params=PARAMS,
        cost_estimate=cost(4),
        name="cut",
    )(initial_path)
    recv = lax.ppermute(other, "gx", swap)
    own = pl.pallas_call(
        own_kernel,
        out_shape=slab(rows),
        in_specs=[hbm],
        out_specs=VMEM,
        scratch_shapes=[pltpu.VMEM(part, jnp.float32), pltpu.SemaphoreType.DMA((tiles,))],
        compiler_params=PARAMS,
        cost_estimate=cost(18),
        name="own",
    )(initial_path)
    known = [0]
    for n in CHUNKS:
        known.append(known[-1] + n)
    sends = [[(a, b - a), (rows - b, b - a)] for a, b in zip(known, known[1:])]
    made = [[], [], []] + [[] for _ in CHUNKS]
    for j, some in enumerate(sends):
        made[max(0, j - LEAD)] += some
    whole, *near = pl.pallas_call(
        functools.partial(first_kernel, rows, made[0]),
        out_shape=[slab(rows)] + [slab(n) for _, n in made[0]],
        in_specs=[VMEM] * 2,
        out_specs=[VMEM] * (1 + len(made[0])),
        compiler_params=PARAMS,
        cost_estimate=cost(18),
        name="first",
    )(own, recv)
    along_chain = []
    for c in range(chains - 1):
        along_chain += [(2 * c + 1, 2 * c + 2), (2 * c + 2, 2 * c + 1)]
    from_partner, from_chain = [], []

    def exchange(piece):
        from_chain.append(lax.ppermute(piece, ("chain", "gx"), along_chain))
        from_partner.append(lax.ppermute(piece, "gx", swap))

    def halos_of(edges):
        for low, high in zip(edges[::2], edges[1::2]):
            halos.append((
                lax.ppermute(high, "gy", ring("gy", 1)),
                lax.ppermute(low, "gy", ring("gy", -1)),
            ))

    halos = []
    halos_of(near)
    inner = pl.pallas_call(
        functools.partial(inner_kernel, rows, made[1]),
        out_shape=[slab(rows - 2 * m) for m in range(1, FIELD + 1)] + [slab(n) for _, n in made[1]],
        in_specs=[VMEM],
        out_specs=[VMEM] * (FIELD + len(made[1])),
        compiler_params=PARAMS,
        cost_estimate=cost(126),
        name="inner",
    )(whole)
    levels = [whole] + list(inner[: FIELD - 1])
    halos_of(inner[FIELD:])
    pieces = [inner[FIELD - 1]]
    exchange(pieces[0])
    segments = [[(FIELD, rows - 2 * FIELD, 0)]]
    for j, (a, b) in enumerate(zip(known, known[1:])):
        beyond = max(0, b - FIELD)
        kept = b - a - beyond
        fields = [slab(2 * n) for n in (kept, beyond) if n]
        buffers = [(2 * (b - a + context(m)), planes, SUB, nz) for m in range(FIELD)]
        last = b == REACH
        ahead = made[j + 2]
        outs = [slab(n) for _, n in ahead] + fields
        if not last:
            outs += [slab(shape[0]) for shape in buffers]
        early = from_chain[j - 1 : j] if j else []
        done = pl.pallas_call(
            functools.partial(edge_kernel, rows, a, b, ahead, len(early)),
            out_shape=outs,
            in_specs=[VMEM] * (FIELD + 3 + len(early)),
            out_specs=[VMEM] * len(outs),
            scratch_shapes=[pltpu.VMEM(shape, jnp.float32) for shape in buffers] if last else [],
            compiler_params=PARAMS,
            cost_estimate=cost(2 * FIELD * (b - a)),
            name="edge",
        )(whole, *halos[j], *levels, *early)
        halos_of(done[: len(ahead)])
        done = done[len(ahead) :]
        if kept:
            pieces.append(done[0])
            exchange(done[0])
            segments.append([(FIELD - a - kept, kept, 0), (rows - FIELD + a, kept, kept)])
        levels = list(done[len(fields) :])
        beyond_rows = done[len(fields) - 1]

    chemical = pl.pallas_call(
        functools.partial(chemical_kernel, rows, segments),
        out_shape=[slab(p.shape[0]) for p in pieces],
        in_specs=[VMEM] * (1 + len(pieces)),
        out_specs=[VMEM] * len(pieces),
        scratch_shapes=[
            pltpu.VMEM((rows + 4, planes, SUB, nz), jnp.float32),
            pltpu.VMEM((rows + 2, planes, SUB, nz), jnp.float32),
        ],
        compiler_params=PARAMS,
        cost_estimate=cost(2 * rows),
        name="chemical",
    )(beyond_rows, *pieces)
    mine, halfway, total = [], [], None
    for some in (slice(0, -1), slice(-1, None)):
        n = len(pieces[some])
        before = [] if total is None else [total]
        kernel = functools.partial(sums_kernel, n, LANES)
        total, *outs = pl.pallas_call(
            kernel if before else functools.partial(kernel, None),
            out_shape=[jax.ShapeDtypeStruct((4, SUB, LANES), jnp.float32)]
            + [slab(p.shape[0]) for p in pieces[some] for _ in range(2)],
            in_specs=[VMEM] * (4 * n + len(before)),
            out_specs=[VMEM] * (1 + 2 * n),
            compiler_params=PARAMS,
            cost_estimate=cost(rows // 2),
            name="sums",
        )(*before, *pieces[some], *from_partner[some], *from_chain[some], *chemical[some])
        mine += outs[::2]
        halfway += [lax.ppermute(send, "gx", swap) for send in outs[1::2]]
    pairs = [
        pl.pallas_call(
            functools.partial(layout_kernel, segments, low),
            out_shape=jax.ShapeDtypeStruct((2, half, rows, nz), jnp.float32),
            in_specs=[VMEM] * len(some),
            out_specs=VMEM,
            scratch_shapes=[pltpu.VMEM((2, *part), jnp.float32), pltpu.SemaphoreType.DMA((2, tiles))],
            compiler_params=PARAMS,
            cost_estimate=cost(rows),
            name="layout",
        )(*some)
        for low, some in ((0, mine), (SUB // 2, halfway))
    ]
    total = total_over(total, "gy", pairs)
    other = lax.ppermute(total, "gx", swap)
    out = []
    for own, sums, pair in ((True, total, pairs[0]), (False, other, pairs[1])):
        out = [pl.pallas_call(
            functools.partial(last_kernel, cells, own),
            out_shape=jax.ShapeDtypeStruct(initial_path.shape, jnp.float32),
            in_specs=[VMEM] * 2 + [hbm] * len(out),
            out_specs=hbm,
            scratch_shapes=[pltpu.VMEM((half, rows, nz), jnp.float32), pltpu.SemaphoreType.DMA((BLOCKS,))],
            input_output_aliases={2: 0} if out else {},
            compiler_params=PARAMS,
            cost_estimate=cost(rows),
            name="last",
        )(sums, pair, *out)]
    return out[0]


def solution(mesh):
    return jax.shard_map(
        per_device,
        mesh=mesh,
        in_specs=(P("chain", "gx", "gy", None),),
        out_specs=P("chain", "gx", "gy", None),
        check_vma=False,
    )
```

```python
import functools

import jax
import jax.numpy as jnp
from jax import lax
from jax.experimental import pallas as pl
from jax.experimental.pallas import tpu as pltpu
from jax.sharding import PartitionSpec as P

RELAX = 3

spacing = 0.7853981633974483
undercool = -0.25
time_step = 0.00025
step_size = 0.002
stiffness = 0.5
epsilon = 1e-06

SUB = 8
LANES = 128
BLOCKS = 4
LAPS = 3
FIELD = LAPS * RELAX
REACH = FIELD + 2
LEAD = 2
CHUNKS = (4, 3, 2, 2)

VMEM = pl.BlockSpec(memory_space=pltpu.VMEM)
SCALE = 1.0


def cost(rows):
    return pl.CostEstimate(flops=0, bytes_accessed=int(SCALE * 130000 * rows), transcendentals=0)


PARAMS = pltpu.CompilerParams(vmem_limit_bytes=8 << 20)


def neighbours(ref, i, side=None):
    c = ref[i]
    up = jnp.concatenate([c[1:], pltpu.roll(c[:1], SUB - 1, 1)], axis=0)
    down = jnp.concatenate([pltpu.roll(c[-1:], 1, 1), c[:-1]], axis=0)
    nz = c.shape[-1]
    if side is None:
        side = pltpu.roll(c, 1, 2) + pltpu.roll(c, nz - 1, 2)
    return (ref[i - 1] + ref[i + 1]) + (up + down) + side - 6.0 * c


def potential_row(v, w, d):
    h2 = spacing * spacing
    return v * ((1.0 + undercool) + v * v) + (2.0 / h2) * w + (1.0 / (h2 * h2)) * d


def context(m):
    return LAPS if m % LAPS == 0 else 2


def level_row(levels, m, y, side=None):
    below, off = levels[m - 1]
    d = neighbours(below, y + off, side)
    kind = m % LAPS
    if kind == 1:
        return d
    w = below[y + off]
    ref, off = levels[m - 2 if kind == 2 else m - LAPS]
    v = ref[y + off]
    if kind == 2:
        return potential_row(v, w, d)
    return v + (time_step / (spacing * spacing)) * d


def ring_matrix(nz):
    apart = jnp.abs(lax.broadcasted_iota(jnp.int32, (nz, nz), 0) - lax.broadcasted_iota(jnp.int32, (nz, nz), 1))
    return jnp.where((apart == 1) | (apart == nz - 1), 1.0, 0.0).astype(jnp.bfloat16)


def side_sums(ref, start, count, ring):
    v = ref[pl.ds(start, count)]
    flat = v.reshape(-1, v.shape[-1])
    high = flat.astype(jnp.bfloat16)
    low = (flat - high.astype(jnp.float32)).astype(jnp.bfloat16)
    total = jnp.dot(high, ring, preferred_element_type=jnp.float32)
    total = total + jnp.dot(low, ring, preferred_element_type=jnp.float32)
    return total.reshape(v.shape)


def rows_of(levels, m, start, stop, into, ring=None):
    count = stop[0] - start[0]
    sums = None
    if ring is not None:
        below, off = levels[1][m - 1]
        sums = side_sums(below, start[1] + off, count, ring)
    for i in range(count):
        for side in range(2):
            ref, off = into[side]
            y = start[side] + i
            ref[y + off] = level_row(levels[side], m, y, sums[i] if side and ring is not None else None)


def cut_kernel(whole_ref, half_ref, sems):
    lanes = half_ref.shape[-1]
    copies = []
    for z in range(half_ref.shape[0]):
        part = whole_ref.at[1 - lax.axis_index("gx"), :, :, pl.ds(z * lanes, lanes)]
        copies.append(pltpu.make_async_copy(part, half_ref.at[z], sems.at[z]))
        copies[-1].start()
    for copy in copies:
        copy.wait()


def own_kernel(whole_ref, slab_ref, half_ref, sems):
    tiles, half, rows, lanes = half_ref.shape
    planes = slab_ref.shape[1]
    copies = []
    for z in range(tiles):
        part = whole_ref.at[lax.axis_index("gx"), :, :, pl.ds(z * lanes, lanes)]
        copies.append(pltpu.make_async_copy(part, half_ref.at[z], sems.at[z]))
        copies[-1].start()
    for copy in copies:
        copy.wait()
    flat = half_ref.reshape(tiles, half * rows, lanes)
    h = SUB // 2

    def body(y, carry):
        for r in range(planes):
            where = pl.ds(r * rows + y, h, stride=planes * rows)
            for z in range(tiles):
                slab_ref[y, r, :h, z * lanes : (z + 1) * lanes] = flat[z, where, :]
        return carry

    lax.fori_loop(0, rows, body, 0)


def first_kernel(rows, sends, own_ref, recv_ref, *refs):
    slab_ref, pieces = refs[0], refs[1:]
    tiles, half, _, lanes = recv_ref.shape
    planes = slab_ref.shape[1]
    flat = recv_ref.reshape(tiles, half * rows, lanes)
    h = SUB // 2

    def row(y):
        for r in range(planes):
            where = pl.ds(r * rows + y, h, stride=planes * rows)
            for z in range(tiles):
                at = slice(z * lanes, (z + 1) * lanes)
                value = jnp.concatenate([own_ref[y, r, :h, at], flat[z, where, :]], axis=0)
                slab_ref[y, r, :, at] = value
                yield r, at, value

    def plain(y, carry):
        for _ in row(y):
            pass
        return carry

    done = 0
    for start, count, piece in sorted(((*send, piece) for send, piece in zip(sends, pieces)), key=lambda s: s[0]):
        if start > done:
            lax.fori_loop(done, start, plain, 0)

        def body(i, carry, start=start, piece=piece):
            for r, at, value in row(start + i):
                piece[i, r, :, at] = value
            return carry

        lax.fori_loop(0, count, body, 0)
        done = start + count
    if rows > done:
        lax.fori_loop(done, rows, plain, 0)


def send_rows(sends, slab_ref, pieces):
    for piece, (start, count) in zip(pieces, sends):
        for i in range(count):
            piece[i] = slab_ref[start + i]


def inner_kernel(rows, sends, slab_ref, *refs):
    outs = refs[:FIELD]
    send_rows(sends, slab_ref, refs[FIELD:])
    levels = [(slab_ref, 0)] + [(ref, -m) for m, ref in enumerate(outs, 1)]
    for m in range(1, FIELD + 1):
        count = (rows - 2 * m) // 2
        start, stop = (m, m + count), (m + count, rows - m)
        rows_of((levels, levels), m, start, stop, (levels[m], levels[m]))


def edge_kernel(rows, before, after, sends, early, slab_ref, low_ref, high_ref, *refs):
    count = after - before
    ring = ring_matrix(low_ref.shape[-1])
    n = len(sends)
    refs = refs[:FIELD] + refs[FIELD + early :]
    send_rows(sends, slab_ref, refs[FIELD : FIELD + n])
    refs = refs[:FIELD] + refs[FIELD + n :]
    past, levels = refs[:FIELD], refs[-FIELD:]
    fields = refs[FIELD:-FIELD]
    sides = ([], [])
    for m, (old, new) in enumerate(zip(past, levels)):
        c = context(m)
        total = count + c
        for i in range(c):
            new[count + i] = old[i]
            new[total + i] = old[old.shape[0] - c + i]
        sides[0].append((new, after - m))
        sides[1].append((new, total + c - (rows - m + before)))

    def fill(i, carry):
        levels[0][i] = low_ref[i]
        levels[0][count + 2 * context(0) + i] = high_ref[i]
        return carry

    lax.fori_loop(0, count, fill, 0)
    for m in range(1, FIELD):
        start = (m - after, rows - m + before)
        stop = (m - before, rows - m + after)
        rows_of(sides, m, start, stop, (sides[0][m], sides[1][m]), ring)
    beyond = max(0, after - FIELD)
    kept = count - beyond
    if kept:
        low = FIELD - after + beyond
        high = rows - FIELD + before
        into = ((fields[0], -low), (fields[0], kept - high))
        rows_of(sides, FIELD, (low, high), (low + kept, high + kept), into, ring)
    if beyond:
        into = ((fields[-1], beyond), (fields[-1], beyond - rows))
        rows_of(sides, FIELD, (-beyond, rows), (0, rows + beyond), into, ring)


def keeping(gx):
    image = 2 * lax.axis_index("chain") + gx
    return jnp.logical_or(image == 0, image == 2 * lax.axis_size("chain") - 1)


def chemical_kernel(rows, segments, halo_ref, *refs):
    n = len(segments)
    pieces, outs = refs[:n], refs[n : 2 * n]
    field_ref, w_ref = refs[2 * n :]
    for i in range(2):
        field_ref[i] = halo_ref[i]
        field_ref[rows + 2 + i] = halo_ref[2 + i]
    for parts, piece in zip(segments, pieces):
        for start, count, first in parts:
            for i in range(count):
                field_ref[2 + start + i] = piece[first + i]
    for i in range(rows + 2):
        w_ref[i] = neighbours(field_ref, i + 1)
    for parts, out in zip(segments, outs):
        for start, count, first in parts:
            for i in range(count):
                y = start + i
                out[first + i] = potential_row(field_ref[y + 2], w_ref[y + 1], neighbours(w_ref, y + 1))


def sums_kernel(n, lanes, before_ref, *refs):
    sums_ref, outs = refs[4 * n], refs[4 * n + 1 :]
    keep = keeping(lax.axis_index("gx"))
    planes, nz = refs[0].shape[1], refs[0].shape[3]

    def fold(a):
        return sum(a[r, :, z : z + lanes] for r in range(planes) for z in range(0, nz, lanes))

    low = lax.broadcasted_iota(jnp.int32, (planes, SUB, nz), 1) < SUB // 2
    totals = [before_ref[q] for q in range(4)] if before_ref is not None else [jnp.zeros((SUB, lanes), jnp.float32)] * 4
    for j in range(n):
        piece, partner, chain, chemical = refs[j : 4 * n : n]
        mine, send = outs[2 * j], outs[2 * j + 1]

        def body(i, totals, piece=piece, partner=partner, chain=chain, chemical=chemical, mine=mine, send=send):
            f, a, b, chem = piece[i], partner[i], chain[i], chemical[i]
            t = a - b
            fr = pltpu.roll(f, SUB // 2, 1)
            cr = pltpu.roll(chem, SUB // 2, 1)
            da, db = a - fr, b - fr
            g = jnp.where(keep, f, f - step_size * chem)
            mine[i] = jnp.where(low, g, t)
            send[i] = jnp.where(low, t, g)
            parts = (fold(t * t), fold(da * da), fold(db * db), fold(cr * t))
            return tuple(total + part for total, part in zip(totals, parts))

        totals = lax.fori_loop(0, piece.shape[0], body, tuple(totals))
    for q in range(4):
        sums_ref[q] = totals[q]


def layout_kernel(segments, low, *refs):
    n = len(segments)
    pair_ref, natural, sems = refs[n:]
    _, tiles, half, rows, lanes = natural.shape
    flat = natural.reshape(2, tiles, half * rows, lanes)
    planes = 2 * half // SUB
    h = SUB // 2
    for parts, ref in zip(segments, refs[:n]):
        for start, count, first in parts:
            def body(j, carry, start=start, first=first, ref=ref):
                for r in range(planes):
                    for z in range(tiles):
                        v = ref[first + j, r, :, z * lanes : (z + 1) * lanes]
                        where = pl.ds(r * rows + start + j, h, stride=planes * rows)
                        flat[0, z, where, :] = v[low : low + h]
                        flat[1, z, where, :] = v[h - low : 2 * h - low]
                return carry

            lax.fori_loop(0, count, body, 0)
    copies = []
    for i in range(2):
        for z in range(tiles):
            part = pair_ref.at[i, :, :, pl.ds(z * lanes, lanes)]
            copies.append(pltpu.make_async_copy(natural.at[i, z], part, sems.at[i, z]))
            copies[-1].start()
    for copy in copies:
        copy.wait()


def last_kernel(cells, own, sums_ref, pair_ref, *refs):
    out_ref, whole, sems = refs[-3:]
    half = whole.shape[0]
    gx = lax.axis_index("gx")
    image = gx if own else 1 - gx

    def total(q):
        return jnp.sum(sums_ref[q], keepdims=True) / cells

    scale = lax.rsqrt(total(0) + epsilon)
    spring = stiffness * (jnp.sqrt(total(1) + epsilon) - jnp.sqrt(total(2) + epsilon))
    k = step_size * total(3) * scale * scale + spring * scale
    k = jnp.where(keeping(image), jnp.zeros_like(k), k)
    copies = []
    step = half // BLOCKS
    for i in range(BLOCKS):
        block = pl.ds(i * step, step)
        whole[block] = pair_ref[0, block] + k * pair_ref[1, block]
        copies.append(pltpu.make_async_copy(whole.at[block], out_ref.at[image, block], sems.at[i]))
        copies[-1].start()
    for copy in copies:
        copy.wait()


def ring(axis, distance):
    n = lax.axis_size(axis)
    return [(i, (i + distance) % n) for i in range(n)]


def add_kernel(a_ref, b_ref, *refs):
    refs[-1][...] = a_ref[...] + b_ref[...]


def add(a, b, *beside):
    return pl.pallas_call(
        add_kernel,
        out_shape=jax.ShapeDtypeStruct(a.shape, a.dtype),
        in_specs=[VMEM] * (2 + len(beside)),
        out_specs=VMEM,
        compiler_params=PARAMS,
        cost_estimate=cost(1),
        name="add",
    )(a, b, *beside)


def total_over(value, axis, beside):
    n = lax.axis_size(axis)
    routes = [ring(axis, d) for d in range(1, n)]
    if n & (n - 1) == 0:
        routes = [[(i, i ^ d) for i in range(n)] for d in (1 << b for b in range(n.bit_length() - 1))]
    start = value
    for route in routes:
        last = route is routes[-1]
        moved = lax.ppermute(start if n & (n - 1) else value, axis, route)
        value = add(value, moved, *(beside if last else ()))
    return value


def per_device(initial_path):
    count, half, rows, nz = initial_path.shape
    assert count == lax.axis_size("gx") == 2
    assert rows % 2 == 0 and rows >= 2 * REACH and half % (SUB * BLOCKS) == 0 and nz % LANES == 0
    planes = 2 * half // SUB
    cells = 2 * half * rows * lax.axis_size("gy") * nz
    chains = lax.axis_size("chain")
    swap = [(0, 1), (1, 0)]
    tiles = nz // LANES
    hbm = pl.BlockSpec(memory_space=pl.ANY)

    def slab(n):
        return jax.ShapeDtypeStruct((n, planes, SUB, nz), jnp.float32)

    part = (tiles, half, rows, LANES)
    other = pl.pallas_call(
        cut_kernel,
        out_shape=jax.ShapeDtypeStruct(part, jnp.float32),
        in_specs=[hbm],
        out_specs=VMEM,
        scratch_shapes=[pltpu.SemaphoreType.DMA((tiles,))],
        compiler_params=PARAMS,
        cost_estimate=cost(4),
        name="cut",
    )(initial_path)
    recv = lax.ppermute(other, "gx", swap)
    own = pl.pallas_call(
        own_kernel,
        out_shape=slab(rows),
        in_specs=[hbm],
        out_specs=VMEM,
        scratch_shapes=[pltpu.VMEM(part, jnp.float32), pltpu.SemaphoreType.DMA((tiles,))],
        compiler_params=PARAMS,
        cost_estimate=cost(18),
        name="own",
    )(initial_path)
    known = [0]
    for n in CHUNKS:
        known.append(known[-1] + n)
    sends = [[(a, b - a), (rows - b, b - a)] for a, b in zip(known, known[1:])]
    made = [[], [], []] + [[] for _ in CHUNKS]
    for j, some in enumerate(sends):
        made[max(0, j - LEAD)] += some
    whole, *near = pl.pallas_call(
        functools.partial(first_kernel, rows, made[0]),
        out_shape=[slab(rows)] + [slab(n) for _, n in made[0]],
        in_specs=[VMEM] * 2,
        out_specs=[VMEM] * (1 + len(made[0])),
        compiler_params=PARAMS,
        cost_estimate=cost(18),
        name="first",
    )(own, recv)
    along_chain = []
    for c in range(chains - 1):
        along_chain += [(2 * c + 1, 2 * c + 2), (2 * c + 2, 2 * c + 1)]
    from_partner, from_chain = [], []

    def exchange(piece):
        from_chain.append(lax.ppermute(piece, ("chain", "gx"), along_chain))
        from_partner.append(lax.ppermute(piece, "gx", swap))

    def halos_of(edges):
        for low, high in zip(edges[::2], edges[1::2]):
            halos.append((
                lax.ppermute(high, "gy", ring("gy", 1)),
                lax.ppermute(low, "gy", ring("gy", -1)),
            ))

    halos = []
    halos_of(near)
    inner = pl.pallas_call(
        functools.partial(inner_kernel, rows, made[1]),
        out_shape=[slab(rows - 2 * m) for m in range(1, FIELD + 1)] + [slab(n) for _, n in made[1]],
        in_specs=[VMEM],
        out_specs=[VMEM] * (FIELD + len(made[1])),
        compiler_params=PARAMS,
        cost_estimate=cost(126),
        name="inner",
    )(whole)
    levels = [whole] + list(inner[: FIELD - 1])
    halos_of(inner[FIELD:])
    pieces = [inner[FIELD - 1]]
    exchange(pieces[0])
    segments = [[(FIELD, rows - 2 * FIELD, 0)]]
    for j, (a, b) in enumerate(zip(known, known[1:])):
        beyond = max(0, b - FIELD)
        kept = b - a - beyond
        fields = [slab(2 * n) for n in (kept, beyond) if n]
        buffers = [(2 * (b - a + context(m)), planes, SUB, nz) for m in range(FIELD)]
        last = b == REACH
        ahead = made[j + 2]
        outs = [slab(n) for _, n in ahead] + fields
        if not last:
            outs += [slab(shape[0]) for shape in buffers]
        early = from_chain[j - 1 : j] if j else []
        done = pl.pallas_call(
            functools.partial(edge_kernel, rows, a, b, ahead, len(early)),
            out_shape=outs,
            in_specs=[VMEM] * (FIELD + 3 + len(early)),
            out_specs=[VMEM] * len(outs),
            scratch_shapes=[pltpu.VMEM(shape, jnp.float32) for shape in buffers] if last else [],
            compiler_params=PARAMS,
            cost_estimate=cost(2 * FIELD * (b - a)),
            name="edge",
        )(whole, *halos[j], *levels, *early)
        halos_of(done[: len(ahead)])
        done = done[len(ahead) :]
        if kept:
            pieces.append(done[0])
            exchange(done[0])
            segments.append([(FIELD - a - kept, kept, 0), (rows - FIELD + a, kept, kept)])
        levels = list(done[len(fields) :])
        beyond_rows = done[len(fields) - 1]

    chemical = pl.pallas_call(
        functools.partial(chemical_kernel, rows, segments),
        out_shape=[slab(p.shape[0]) for p in pieces],
        in_specs=[VMEM] * (1 + len(pieces)),
        out_specs=[VMEM] * len(pieces),
        scratch_shapes=[
            pltpu.VMEM((rows + 4, planes, SUB, nz), jnp.float32),
            pltpu.VMEM((rows + 2, planes, SUB, nz), jnp.float32),
        ],
        compiler_params=PARAMS,
        cost_estimate=cost(2 * rows),
        name="chemical",
    )(beyond_rows, *pieces)
    mine, halfway, total = [], [], None
    for some in (slice(0, -1), slice(-1, None)):
        n = len(pieces[some])
        before = [] if total is None else [total]
        kernel = functools.partial(sums_kernel, n, LANES)
        total, *outs = pl.pallas_call(
            kernel if before else functools.partial(kernel, None),
            out_shape=[jax.ShapeDtypeStruct((4, SUB, LANES), jnp.float32)]
            + [slab(p.shape[0]) for p in pieces[some] for _ in range(2)],
            in_specs=[VMEM] * (4 * n + len(before)),
            out_specs=[VMEM] * (1 + 2 * n),
            compiler_params=PARAMS,
            cost_estimate=cost(rows // 2),
            name="sums",
        )(*before, *pieces[some], *from_partner[some], *from_chain[some], *chemical[some])
        mine += outs[::2]
        halfway += [lax.ppermute(send, "gx", swap) for send in outs[1::2]]
    pairs = [
        pl.pallas_call(
            functools.partial(layout_kernel, segments, low),
            out_shape=jax.ShapeDtypeStruct((2, half, rows, nz), jnp.float32),
            in_specs=[VMEM] * len(some),
            out_specs=VMEM,
            scratch_shapes=[pltpu.VMEM((2, *part), jnp.float32), pltpu.SemaphoreType.DMA((2, tiles))],
            compiler_params=PARAMS,
            cost_estimate=cost(rows),
            name="layout",
        )(*some)
        for low, some in ((0, mine), (SUB // 2, halfway))
    ]
    total = total_over(total, "gy", pairs)
    other = lax.ppermute(total, "gx", swap)
    out = []
    for own, sums, pair in ((True, total, pairs[0]), (False, other, pairs[1])):
        out = [pl.pallas_call(
            functools.partial(last_kernel, cells, own),
            out_shape=jax.ShapeDtypeStruct(initial_path.shape, jnp.float32),
            in_specs=[VMEM] * 2 + [hbm] * len(out),
            out_specs=hbm,
            scratch_shapes=[pltpu.VMEM((half, rows, nz), jnp.float32), pltpu.SemaphoreType.DMA((BLOCKS,))],
            input_output_aliases={2: 0} if out else {},
            compiler_params=PARAMS,
            cost_estimate=cost(rows),
            name="last",
        )(sums, pair, *out)]
    return out[0]


def solution(mesh):
    return jax.shard_map(
        per_device,
        mesh=mesh,
        in_specs=(P("chain", "gx", "gy", None),),
        out_specs=P("chain", "gx", "gy", None),
        check_vma=False,
    )
```

```python
import functools

import jax
import jax.numpy as jnp
from jax import lax
from jax.experimental import pallas as pl
from jax.experimental.pallas import tpu as pltpu
from jax.sharding import PartitionSpec as P

RELAX = 3

spacing = 0.7853981633974483
undercool = -0.25
time_step = 0.00025
step_size = 0.002
stiffness = 0.5
epsilon = 1e-06

SUB = 8
LANES = 128
BLOCKS = 4
LAPS = 3
FIELD = LAPS * RELAX
REACH = FIELD + 2
LEAD = 2
CHUNKS = (4, 3, 2, 2)

VMEM = pl.BlockSpec(memory_space=pltpu.VMEM)
SCALE = 1.0


def cost(rows):
    return pl.CostEstimate(flops=0, bytes_accessed=int(SCALE * 130000 * rows), transcendentals=0)


PARAMS = pltpu.CompilerParams(vmem_limit_bytes=8 << 20)


def neighbours(ref, i, side=None):
    c = ref[i]
    up = jnp.concatenate([c[1:], pltpu.roll(c[:1], SUB - 1, 1)], axis=0)
    down = jnp.concatenate([pltpu.roll(c[-1:], 1, 1), c[:-1]], axis=0)
    nz = c.shape[-1]
    if side is None:
        side = pltpu.roll(c, 1, 2) + pltpu.roll(c, nz - 1, 2)
    return (ref[i - 1] + ref[i + 1]) + (up + down) + side - 6.0 * c


def potential_row(v, w, d):
    h2 = spacing * spacing
    return v * ((1.0 + undercool) + v * v) + (2.0 / h2) * w + (1.0 / (h2 * h2)) * d


def context(m):
    return LAPS if m % LAPS == 0 else 2


def level_row(levels, m, y, side=None):
    below, off = levels[m - 1]
    d = neighbours(below, y + off, side)
    kind = m % LAPS
    if kind == 1:
        return d
    w = below[y + off]
    ref, off = levels[m - 2 if kind == 2 else m - LAPS]
    v = ref[y + off]
    if kind == 2:
        return potential_row(v, w, d)
    return v + (time_step / (spacing * spacing)) * d


def ring_matrix(nz):
    apart = jnp.abs(lax.broadcasted_iota(jnp.int32, (nz, nz), 0) - lax.broadcasted_iota(jnp.int32, (nz, nz), 1))
    return jnp.where((apart == 1) | (apart == nz - 1), 1.0, 0.0).astype(jnp.bfloat16)


def side_sums(ref, start, count, ring):
    v = ref[pl.ds(start, count)]
    flat = v.reshape(-1, v.shape[-1])
    high = flat.astype(jnp.bfloat16)
    low = (flat - high.astype(jnp.float32)).astype(jnp.bfloat16)
    total = jnp.dot(high, ring, preferred_element_type=jnp.float32)
    total = total + jnp.dot(low, ring, preferred_element_type=jnp.float32)
    return total.reshape(v.shape)


def rows_of(levels, m, start, stop, into, ring=None):
    count = stop[0] - start[0]
    sums = None
    if ring is not None:
        below, off = levels[1][m - 1]
        sums = side_sums(below, start[1] + off, count, ring)
    for i in range(count):
        for side in range(2):
            ref, off = into[side]
            y = start[side] + i
            ref[y + off] = level_row(levels[side], m, y, sums[i] if side and ring is not None else None)


def cut_kernel(whole_ref, half_ref, sems):
    lanes = half_ref.shape[-1]
    copies = []
    for z in range(half_ref.shape[0]):
        part = whole_ref.at[1 - lax.axis_index("gx"), :, :, pl.ds(z * lanes, lanes)]
        copies.append(pltpu.make_async_copy(part, half_ref.at[z], sems.at[z]))
        copies[-1].start()
    for copy in copies:
        copy.wait()


def own_kernel(whole_ref, slab_ref, half_ref, sems):
    tiles, half, rows, lanes = half_ref.shape
    planes = slab_ref.shape[1]
    copies = []
    for z in range(tiles):
        part = whole_ref.at[lax.axis_index("gx"), :, :, pl.ds(z * lanes, lanes)]
        copies.append(pltpu.make_async_copy(part, half_ref.at[z], sems.at[z]))
        copies[-1].start()
    for copy in copies:
        copy.wait()
    flat = half_ref.reshape(tiles, half * rows, lanes)
    h = SUB // 2

    def body(y, carry):
        for r in range(planes):
            where = pl.ds(r * rows + y, h, stride=planes * rows)
            for z in range(tiles):
                slab_ref[y, r, :h, z * lanes : (z + 1) * lanes] = flat[z, where, :]
        return carry

    lax.fori_loop(0, rows, body, 0)


def first_kernel(rows, sends, own_ref, recv_ref, *refs):
    slab_ref, pieces = refs[0], refs[1:]
    tiles, half, _, lanes = recv_ref.shape
    planes = slab_ref.shape[1]
    flat = recv_ref.reshape(tiles, half * rows, lanes)
    h = SUB // 2

    def row(y):
        for r in range(planes):
            where = pl.ds(r * rows + y, h, stride=planes * rows)
            for z in range(tiles):
                at = slice(z * lanes, (z + 1) * lanes)
                value = jnp.concatenate([own_ref[y, r, :h, at], flat[z, where, :]], axis=0)
                slab_ref[y, r, :, at] = value
                yield r, at, value

    def plain(y, carry):
        for _ in row(y):
            pass
        return carry

    done = 0
    for start, count, piece in sorted(((*send, piece) for send, piece in zip(sends, pieces)), key=lambda s: s[0]):
        if start > done:
            lax.fori_loop(done, start, plain, 0)

        def body(i, carry, start=start, piece=piece):
            for r, at, value in row(start + i):
                piece[i, r, :, at] = value
            return carry

        lax.fori_loop(0, count, body, 0)
        done = start + count
    if rows > done:
        lax.fori_loop(done, rows, plain, 0)


def send_rows(sends, slab_ref, pieces):
    for piece, (start, count) in zip(pieces, sends):
        for i in range(count):
            piece[i] = slab_ref[start + i]


def inner_kernel(rows, sends, slab_ref, *refs):
    outs = refs[:FIELD]
    ring = ring_matrix(slab_ref.shape[-1])
    send_rows(sends, slab_ref, refs[FIELD:])
    levels = [(slab_ref, 0)] + [(ref, -m) for m, ref in enumerate(outs, 1)]
    for m in range(1, FIELD + 1):
        count = (rows - 2 * m) // 2
        start, stop = (m, m + count), (m + count, rows - m)
        rows_of((levels, levels), m, start, stop, (levels[m], levels[m]), ring)


def edge_kernel(rows, before, after, sends, early, slab_ref, low_ref, high_ref, *refs):
    count = after - before
    ring = ring_matrix(low_ref.shape[-1])
    n = len(sends)
    refs = refs[:FIELD] + refs[FIELD + early :]
    send_rows(sends, slab_ref, refs[FIELD : FIELD + n])
    refs = refs[:FIELD] + refs[FIELD + n :]
    past, levels = refs[:FIELD], refs[-FIELD:]
    fields = refs[FIELD:-FIELD]
    sides = ([], [])
    for m, (old, new) in enumerate(zip(past, levels)):
        c = context(m)
        total = count + c
        for i in range(c):
            new[count + i] = old[i]
            new[total + i] = old[old.shape[0] - c + i]
        sides[0].append((new, after - m))
        sides[1].append((new, total + c - (rows - m + before)))

    def fill(i, carry):
        levels[0][i] = low_ref[i]
        levels[0][count + 2 * context(0) + i] = high_ref[i]
        return carry

    lax.fori_loop(0, count, fill, 0)
    for m in range(1, FIELD):
        start = (m - after, rows - m + before)
        stop = (m - before, rows - m + after)
        rows_of(sides, m, start, stop, (sides[0][m], sides[1][m]), ring)
    beyond = max(0, after - FIELD)
    kept = count - beyond
    if kept:
        low = FIELD - after + beyond
        high = rows - FIELD + before
        into = ((fields[0], -low), (fields[0], kept - high))
        rows_of(sides, FIELD, (low, high), (low + kept, high + kept), into, ring)
    if beyond:
        into = ((fields[-1], beyond), (fields[-1], beyond - rows))
        rows_of(sides, FIELD, (-beyond, rows), (0, rows + beyond), into, ring)


def keeping(gx):
    image = 2 * lax.axis_index("chain") + gx
    return jnp.logical_or(image == 0, image == 2 * lax.axis_size("chain") - 1)


def chemical_kernel(rows, segments, halo_ref, *refs):
    n = len(segments)
    pieces, outs = refs[:n], refs[n : 2 * n]
    field_ref, w_ref = refs[2 * n :]
    for i in range(2):
        field_ref[i] = halo_ref[i]
        field_ref[rows + 2 + i] = halo_ref[2 + i]
    for parts, piece in zip(segments, pieces):
        for start, count, first in parts:
            for i in range(count):
                field_ref[2 + start + i] = piece[first + i]
    for i in range(rows + 2):
        w_ref[i] = neighbours(field_ref, i + 1)
    for parts, out in zip(segments, outs):
        for start, count, first in parts:
            for i in range(count):
                y = start + i
                out[first + i] = potential_row(field_ref[y + 2], w_ref[y + 1], neighbours(w_ref, y + 1))


def sums_kernel(n, lanes, before_ref, *refs):
    sums_ref, outs = refs[4 * n], refs[4 * n + 1 :]
    keep = keeping(lax.axis_index("gx"))
    planes, nz = refs[0].shape[1], refs[0].shape[3]

    def fold(a):
        return sum(a[r, :, z : z + lanes] for r in range(planes) for z in range(0, nz, lanes))

    low = lax.broadcasted_iota(jnp.int32, (planes, SUB, nz), 1) < SUB // 2
    totals = [before_ref[q] for q in range(4)] if before_ref is not None else [jnp.zeros((SUB, lanes), jnp.float32)] * 4
    for j in range(n):
        piece, partner, chain, chemical = refs[j : 4 * n : n]
        mine, send = outs[2 * j], outs[2 * j + 1]

        def body(i, totals, piece=piece, partner=partner, chain=chain, chemical=chemical, mine=mine, send=send):
            f, a, b, chem = piece[i], partner[i], chain[i], chemical[i]
            t = a - b
            fr = pltpu.roll(f, SUB // 2, 1)
            cr = pltpu.roll(chem, SUB // 2, 1)
            da, db = a - fr, b - fr
            g = jnp.where(keep, f, f - step_size * chem)
            mine[i] = jnp.where(low, g, t)
            send[i] = jnp.where(low, t, g)
            parts = (fold(t * t), fold(da * da), fold(db * db), fold(cr * t))
            return tuple(total + part for total, part in zip(totals, parts))

        totals = lax.fori_loop(0, piece.shape[0], body, tuple(totals))
    for q in range(4):
        sums_ref[q] = totals[q]


def layout_kernel(segments, low, *refs):
    n = len(segments)
    pair_ref, natural, sems = refs[n:]
    _, tiles, half, rows, lanes = natural.shape
    flat = natural.reshape(2, tiles, half * rows, lanes)
    planes = 2 * half // SUB
    h = SUB // 2
    for parts, ref in zip(segments, refs[:n]):
        for start, count, first in parts:
            def body(j, carry, start=start, first=first, ref=ref):
                for r in range(planes):
                    for z in range(tiles):
                        v = ref[first + j, r, :, z * lanes : (z + 1) * lanes]
                        where = pl.ds(r * rows + start + j, h, stride=planes * rows)
                        flat[0, z, where, :] = v[low : low + h]
                        flat[1, z, where, :] = v[h - low : 2 * h - low]
                return carry

            lax.fori_loop(0, count, body, 0)
    copies = []
    for i in range(2):
        for z in range(tiles):
            part = pair_ref.at[i, :, :, pl.ds(z * lanes, lanes)]
            copies.append(pltpu.make_async_copy(natural.at[i, z], part, sems.at[i, z]))
            copies[-1].start()
    for copy in copies:
        copy.wait()


def last_kernel(cells, own, sums_ref, pair_ref, *refs):
    out_ref, whole, sems = refs[-3:]
    half = whole.shape[0]
    gx = lax.axis_index("gx")
    image = gx if own else 1 - gx

    def total(q):
        return jnp.sum(sums_ref[q], keepdims=True) / cells

    scale = lax.rsqrt(total(0) + epsilon)
    spring = stiffness * (jnp.sqrt(total(1) + epsilon) - jnp.sqrt(total(2) + epsilon))
    k = step_size * total(3) * scale * scale + spring * scale
    k = jnp.where(keeping(image), jnp.zeros_like(k), k)
    copies = []
    step = half // BLOCKS
    for i in range(BLOCKS):
        block = pl.ds(i * step, step)
        whole[block] = pair_ref[0, block] + k * pair_ref[1, block]
        copies.append(pltpu.make_async_copy(whole.at[block], out_ref.at[image, block], sems.at[i]))
        copies[-1].start()
    for copy in copies:
        copy.wait()


def ring(axis, distance):
    n = lax.axis_size(axis)
    return [(i, (i + distance) % n) for i in range(n)]


def add_kernel(a_ref, b_ref, *refs):
    refs[-1][...] = a_ref[...] + b_ref[...]


def add(a, b, *beside):
    return pl.pallas_call(
        add_kernel,
        out_shape=jax.ShapeDtypeStruct(a.shape, a.dtype),
        in_specs=[VMEM] * (2 + len(beside)),
        out_specs=VMEM,
        compiler_params=PARAMS,
        cost_estimate=cost(1),
        name="add",
    )(a, b, *beside)


def total_over(value, axis, beside):
    n = lax.axis_size(axis)
    routes = [ring(axis, d) for d in range(1, n)]
    if n & (n - 1) == 0:
        routes = [[(i, i ^ d) for i in range(n)] for d in (1 << b for b in range(n.bit_length() - 1))]
    start = value
    for route in routes:
        last = route is routes[-1]
        moved = lax.ppermute(start if n & (n - 1) else value, axis, route)
        value = add(value, moved, *(beside if last else ()))
    return value


def per_device(initial_path):
    count, half, rows, nz = initial_path.shape
    assert count == lax.axis_size("gx") == 2
    assert rows % 2 == 0 and rows >= 2 * REACH and half % (SUB * BLOCKS) == 0 and nz % LANES == 0
    planes = 2 * half // SUB
    cells = 2 * half * rows * lax.axis_size("gy") * nz
    chains = lax.axis_size("chain")
    swap = [(0, 1), (1, 0)]
    tiles = nz // LANES
    hbm = pl.BlockSpec(memory_space=pl.ANY)

    def slab(n):
        return jax.ShapeDtypeStruct((n, planes, SUB, nz), jnp.float32)

    part = (tiles, half, rows, LANES)
    other = pl.pallas_call(
        cut_kernel,
        out_shape=jax.ShapeDtypeStruct(part, jnp.float32),
        in_specs=[hbm],
        out_specs=VMEM,
        scratch_shapes=[pltpu.SemaphoreType.DMA((tiles,))],
        compiler_params=PARAMS,
        cost_estimate=cost(4),
        name="cut",
    )(initial_path)
    recv = lax.ppermute(other, "gx", swap)
    own = pl.pallas_call(
        own_kernel,
        out_shape=slab(rows),
        in_specs=[hbm],
        out_specs=VMEM,
        scratch_shapes=[pltpu.VMEM(part, jnp.float32), pltpu.SemaphoreType.DMA((tiles,))],
        compiler_params=PARAMS,
        cost_estimate=cost(18),
        name="own",
    )(initial_path)
    known = [0]
    for n in CHUNKS:
        known.append(known[-1] + n)
    sends = [[(a, b - a), (rows - b, b - a)] for a, b in zip(known, known[1:])]
    made = [[], [], []] + [[] for _ in CHUNKS]
    for j, some in enumerate(sends):
        made[max(0, j - LEAD)] += some
    whole, *near = pl.pallas_call(
        functools.partial(first_kernel, rows, made[0]),
        out_shape=[slab(rows)] + [slab(n) for _, n in made[0]],
        in_specs=[VMEM] * 2,
        out_specs=[VMEM] * (1 + len(made[0])),
        compiler_params=PARAMS,
        cost_estimate=cost(18),
        name="first",
    )(own, recv)
    along_chain = []
    for c in range(chains - 1):
        along_chain += [(2 * c + 1, 2 * c + 2), (2 * c + 2, 2 * c + 1)]
    from_partner, from_chain = [], []

    def exchange(piece):
        from_chain.append(lax.ppermute(piece, ("chain", "gx"), along_chain))
        from_partner.append(lax.ppermute(piece, "gx", swap))

    def halos_of(edges):
        for low, high in zip(edges[::2], edges[1::2]):
            halos.append((
                lax.ppermute(high, "gy", ring("gy", 1)),
                lax.ppermute(low, "gy", ring("gy", -1)),
            ))

    halos = []
    halos_of(near)
    inner = pl.pallas_call(
        functools.partial(inner_kernel, rows, made[1]),
        out_shape=[slab(rows - 2 * m) for m in range(1, FIELD + 1)] + [slab(n) for _, n in made[1]],
        in_specs=[VMEM],
        out_specs=[VMEM] * (FIELD + len(made[1])),
        compiler_params=PARAMS,
        cost_estimate=cost(126),
        name="inner",
    )(whole)
    levels = [whole] + list(inner[: FIELD - 1])
    halos_of(inner[FIELD:])
    pieces = [inner[FIELD - 1]]
    exchange(pieces[0])
    segments = [[(FIELD, rows - 2 * FIELD, 0)]]
    for j, (a, b) in enumerate(zip(known, known[1:])):
        beyond = max(0, b - FIELD)
        kept = b - a - beyond
        fields = [slab(2 * n) for n in (kept, beyond) if n]
        buffers = [(2 * (b - a + context(m)), planes, SUB, nz) for m in range(FIELD)]
        last = b == REACH
        ahead = made[j + 2]
        outs = [slab(n) for _, n in ahead] + fields
        if not last:
            outs += [slab(shape[0]) for shape in buffers]
        early = from_chain[j - 1 : j] if j else []
        done = pl.pallas_call(
            functools.partial(edge_kernel, rows, a, b, ahead, len(early)),
            out_shape=outs,
            in_specs=[VMEM] * (FIELD + 3 + len(early)),
            out_specs=[VMEM] * len(outs),
            scratch_shapes=[pltpu.VMEM(shape, jnp.float32) for shape in buffers] if last else [],
            compiler_params=PARAMS,
            cost_estimate=cost(2 * FIELD * (b - a)),
            name="edge",
        )(whole, *halos[j], *levels, *early)
        halos_of(done[: len(ahead)])
        done = done[len(ahead) :]
        if kept:
            pieces.append(done[0])
            exchange(done[0])
            segments.append([(FIELD - a - kept, kept, 0), (rows - FIELD + a, kept, kept)])
        levels = list(done[len(fields) :])
        beyond_rows = done[len(fields) - 1]

    chemical = pl.pallas_call(
        functools.partial(chemical_kernel, rows, segments),
        out_shape=[slab(p.shape[0]) for p in pieces],
        in_specs=[VMEM] * (1 + len(pieces)),
        out_specs=[VMEM] * len(pieces),
        scratch_shapes=[
            pltpu.VMEM((rows + 4, planes, SUB, nz), jnp.float32),
            pltpu.VMEM((rows + 2, planes, SUB, nz), jnp.float32),
        ],
        compiler_params=PARAMS,
        cost_estimate=cost(2 * rows),
        name="chemical",
    )(beyond_rows, *pieces)
    mine, halfway, total = [], [], None
    for some in (slice(0, -1), slice(-1, None)):
        n = len(pieces[some])
        before = [] if total is None else [total]
        kernel = functools.partial(sums_kernel, n, LANES)
        total, *outs = pl.pallas_call(
            kernel if before else functools.partial(kernel, None),
            out_shape=[jax.ShapeDtypeStruct((4, SUB, LANES), jnp.float32)]
            + [slab(p.shape[0]) for p in pieces[some] for _ in range(2)],
            in_specs=[VMEM] * (4 * n + len(before)),
            out_specs=[VMEM] * (1 + 2 * n),
            compiler_params=PARAMS,
            cost_estimate=cost(rows // 2),
            name="sums",
        )(*before, *pieces[some], *from_partner[some], *from_chain[some], *chemical[some])
        mine += outs[::2]
        halfway += [lax.ppermute(send, "gx", swap) for send in outs[1::2]]
    pairs = [
        pl.pallas_call(
            functools.partial(layout_kernel, segments, low),
            out_shape=jax.ShapeDtypeStruct((2, half, rows, nz), jnp.float32),
            in_specs=[VMEM] * len(some),
            out_specs=VMEM,
            scratch_shapes=[pltpu.VMEM((2, *part), jnp.float32), pltpu.SemaphoreType.DMA((2, tiles))],
            compiler_params=PARAMS,
            cost_estimate=cost(rows),
            name="layout",
        )(*some)
        for low, some in ((0, mine), (SUB // 2, halfway))
    ]
    total = total_over(total, "gy", pairs)
    other = lax.ppermute(total, "gx", swap)
    out = []
    for own, sums, pair in ((True, total, pairs[0]), (False, other, pairs[1])):
        out = [pl.pallas_call(
            functools.partial(last_kernel, cells, own),
            out_shape=jax.ShapeDtypeStruct(initial_path.shape, jnp.float32),
            in_specs=[VMEM] * 2 + [hbm] * len(out),
            out_specs=hbm,
            scratch_shapes=[pltpu.VMEM((half, rows, nz), jnp.float32), pltpu.SemaphoreType.DMA((BLOCKS,))],
            input_output_aliases={2: 0} if out else {},
            compiler_params=PARAMS,
            cost_estimate=cost(rows),
            name="last",
        )(sums, pair, *out)]
    return out[0]


def solution(mesh):
    return jax.shard_map(
        per_device,
        mesh=mesh,
        in_specs=(P("chain", "gx", "gy", None),),
        out_specs=P("chain", "gx", "gy", None),
        check_vma=False,
    )
```
